32 devices in a mesh: ens: 2 (over x), tile: 8 (over z, y), lev: 2 (over core).
Axes of the slice: x: 2, y: 2, z: 4, core: 2. Of those that a mesh axis runs over, the one named last changes fastest.
Arguments:
- cotangent: float32 [34, 5, 8, 4, 18432], P(None, None, 'lev', None, ('ens', 'tile')), parts along dimension 4, may hold values from -6 to 6
- stencil_col: int32 [5, 18432], P(None, ('ens', 'tile')), parts along dimension 1, may hold values from 0 to 3071, as said below
- stencil_row: int32 [5, 18432], P(None, ('ens', 'tile')), parts along dimension 1, may hold values from 0 to 2, as said below
- frac_along: float32 [5, 18432], P(None, ('ens', 'tile')), parts along dimension 1, may hold values from 0 to 1
- frac_across: float32 [5, 18432], P(None, ('ens', 'tile')), parts along dimension 1, may hold values from 0 to 1
- owner_map: int32 [16, 8], P(('ens', 'tile')), parts along dimension 0, may hold values from 0 to 7, as said below
Outputs:
- parent_grad: float32 [12, 5, 8, 6, 6144], P(None, None, 'lev', None, ('ens', 'tile')), parts along dimension 4
The draws below stay inside these ranges and needn't reach their ends.
There are 2 independent parts, one for each index of `ens`. The reference program is written for one: setup_inputs(seed, part) draws one part's arguments, and reference() takes and returns one part's arrays. A program takes and returns all parts, laid end to end along the dimension named above; each array names one. Nothing has to cross between parts.
Inputs may be any that keep to these rules, and one draw needn't show every extreme that they name: stencil_col[r, p] - p // 3 is -2, -1 or 0 modulo 3072. stencil_row[r, p] - r // 3 is 0 or 1. `owner_map`: every row is a permutation of 0 to 7.
All inputs are finite; a program needn't handle non-finite values.
Results may differ from the reference program's by a relative error of at most 0.00007.
Values sent between devices are 32-bit elements; how exact they have to be, the bound alone decides.
No kernel may reach another device: no remote copies, remote signals or barrier semaphores. Data moves between devices by JAX's collectives and lax.ppermute only.
A program may use at most 448 MiB of HBM per device.

```python
import jax
import jax.numpy as jnp
from jax import lax

FLD = 5
LEV = 8
ZONE = 5
FORCED = 4
PROWS = 6
NT = 12
STEPS_PER = 3
NSTEP = 34
BW = 48
PERIM = 9216
PPERIM = 3072
N_TILE = 8


def draw_stencil_col(key, part):
    key = jax.random.fold_in(key, 11)
    jitter = jax.random.randint(key, (ZONE, PERIM), -2, 1)
    jitter = jitter.at[:, 0].set(0).at[:, PERIM - 1].set(0)
    position = jnp.arange(PERIM, dtype=jnp.int32) // 3
    return ((position[None, :] + jitter) % PPERIM).astype(jnp.int32)


def draw_stencil_row(key, part):
    key = jax.random.fold_in(key, 12)
    jitter = jax.random.randint(key, (ZONE, PERIM), 0, 2)
    jitter = jitter.at[0, 0].set(0).at[ZONE - 1, 0].set(1)
    base_row = jnp.arange(ZONE, dtype=jnp.int32) // 3
    return (base_row[:, None] + jitter).astype(jnp.int32)


def draw_owner_map(key, part):
    key = jax.random.fold_in(key, 13)
    row_keys = jax.random.split(key, N_TILE)
    return jax.vmap(lambda row_key: jax.random.permutation(row_key, N_TILE))(row_keys).astype(jnp.int32)


def steps_of(own_key, dims, pieces, smallest, largest):
    level, own = 1.0, jax.random.fold_in(own_key, 6)
    for dim, shards_of in pieces:
        heights = jnp.exp(jax.random.uniform(jax.random.fold_in(own, dim), (shards_of,), jnp.float32, smallest / len(pieces), largest / len(pieces)))
        level = level * jnp.repeat(heights, dims[dim] // shards_of).reshape([-1 if axis == dim else 1 for axis in range(len(dims))])
    return level


def centred(key, extent, deviation, bound, cuts=(), kind=jnp.bfloat16):
    drawn = deviation * jax.random.normal(key, extent, jnp.float32)
    if cuts:
        drawn = drawn * steps_of(key, extent, cuts, -0.22, 0.18)
    return jnp.clip(drawn, -bound, bound).astype(kind)


def setup_inputs(seed: int = 0, part: int = 0) -> dict:
    splits = jax.random.split(jax.random.key(seed), 7)
    own_keys = jax.random.split(jax.random.fold_in(splits[6], part), 7)
    cotangent = centred(own_keys[0], (NSTEP, FLD, LEV, FORCED, PERIM), 1.0, 6.0, ((2, 2), (4, 8)), jnp.float32)
    stencil_col = draw_stencil_col(jax.random.fold_in(jax.random.fold_in(splits[6], part), 71), part)
    stencil_row = draw_stencil_row(jax.random.fold_in(jax.random.fold_in(splits[6], part), 71), part)
    frac_along = jnp.clip(1.0 * jax.random.uniform(own_keys[3], (ZONE, PERIM), jnp.float32) ** steps_of(own_keys[3], (ZONE, PERIM), ((1, 8),), -0.2, 0.2), 0.0, 1.0)
    frac_across = jnp.clip(1.0 * jax.random.uniform(own_keys[4], (ZONE, PERIM), jnp.float32) ** steps_of(own_keys[4], (ZONE, PERIM), ((1, 8),), -0.2, 0.2), 0.0, 1.0)
    owner_map = draw_owner_map(jax.random.fold_in(jax.random.fold_in(splits[6], part), 71), part)
    return {"cotangent": cotangent, "stencil_col": stencil_col, "stencil_row": stencil_row, "frac_along": frac_along, "frac_across": frac_across, "owner_map": owner_map}


def lagrange_weights(fraction):
    shifted = fraction + 1.0
    return jnp.stack([-fraction * (fraction - 1.0) * (fraction - 2.0) / 6.0,
                      shifted * (fraction - 1.0) * (fraction - 2.0) / 2.0,
                      -shifted * fraction * (fraction - 2.0) / 2.0,
                      shifted * fraction * (fraction - 1.0) / 6.0], axis=-1)


def zone_factors(row_count):
    rowpos = jnp.arange(row_count)
    relax_factor = jnp.where(rowpos == 0, 0.0, (row_count - rowpos) / (row_count - 1.0)).astype(jnp.float32)
    diffuse = (0.2 * relax_factor).astype(jnp.float32)
    center = jnp.where(rowpos == 0, 1.0, relax_factor + 4.0 * diffuse).astype(jnp.float32)
    return center, diffuse


def time_weights():
    step_pos = jnp.arange(NSTEP).astype(jnp.float32)
    parent = jnp.arange(NT).astype(jnp.float32)
    return jnp.maximum(0.0, 1.0 - jnp.abs(step_pos[None, :] - STEPS_PER * parent[:, None]) / STEPS_PER).astype(jnp.float32)


def vertical(base_term, spread):
    zero_row = jnp.zeros_like(base_term[..., :1, :])
    base_full = jnp.concatenate([base_term, zero_row], axis=-2)
    spread_full = jnp.concatenate([spread, zero_row], axis=-2)
    from_above = jnp.concatenate([zero_row, spread_full[..., :-1, :]], axis=-2)
    from_below = jnp.concatenate([spread_full[..., 1:, :], zero_row], axis=-2)
    return base_full - from_above - from_below


def reference(cotangent, stencil_col, stencil_row, frac_along, frac_across, owner_map):
    center, diffuse = zone_factors(FORCED)
    spread = cotangent * diffuse[:, None]
    base_term = cotangent * center[:, None] - (jnp.roll(spread, 1, axis=-1) + jnp.roll(spread, -1, axis=-1))
    zone_bar = vertical(base_term, spread)
    weights = time_weights()
    folded = jnp.einsum("kt,tflrp->kflrp", weights, zone_bar, precision=lax.Precision.HIGHEST)
    col_weight = lagrange_weights(frac_along)
    row_weight = lagrange_weights(frac_across)
    gradient = jnp.zeros((NT, FLD, LEV, PROWS * PPERIM), jnp.float32)
    for col_tap in range(4):
        for row_tap in range(4):
            target = ((stencil_row + row_tap) * PPERIM + (stencil_col + col_tap) % PPERIM).astype(jnp.int32)
            gradient = gradient.at[..., target].add(folded * (row_weight[..., row_tap] * col_weight[..., col_tap]))
    grid = gradient.reshape(NT, FLD, LEV, PROWS, N_TILE, N_TILE, BW)
    inverse = jnp.argsort(owner_map, axis=1).astype(jnp.int32)
    source = jnp.arange(N_TILE, dtype=jnp.int32)[:, None]
    picked = grid[:, :, :, :, source, inverse, :]
    return jnp.swapaxes(picked, 4, 5).reshape(NT, FLD, LEV, PROWS, PPERIM)
```

```python
import functools

import jax
import jax.numpy as jnp
from jax import lax
from jax.experimental import pallas as pl
from jax.experimental.pallas import tpu as pltpu
from jax.sharding import PartitionSpec as P

PROWS = 6
NT = 12
STEPS_PER = 3
LANES = 128
TAPS = 4
SPILL = 4
SPILL_ROWS = 32
FAR = -(1 << 20)
VMEM_BYTES = 56 << 20


def zone_factors(forced):
    relax = [0.0] + [(forced - r) / (forced - 1.0) for r in range(1, forced)]
    diffuse = [0.2 * value for value in relax]
    center = [1.0] + [relax[r] + 4.0 * diffuse[r] for r in range(1, forced)]
    return center, diffuse


def lagrange_weights(fraction):
    shifted = fraction + 1.0
    return [
        -fraction * (fraction - 1.0) * (fraction - 2.0) / 6.0,
        shifted * (fraction - 1.0) * (fraction - 2.0) / 2.0,
        -shifted * fraction * (fraction - 2.0) / 2.0,
        shifted * fraction * (fraction - 1.0) / 6.0,
    ]


def split_bf16(value):
    high = value.astype(jnp.bfloat16)
    low = (value - high.astype(jnp.float32)).astype(jnp.bfloat16)
    return high, low


def tap_select(distance, weights):
    picked = jnp.where(distance == TAPS - 1, weights[TAPS - 1], 0.0)
    for tap in range(TAPS - 2, -1, -1):
        picked = jnp.where(distance == tap, weights[tap], picked)
    return picked


def first_columns(cols, third, tile_start, total):
    offset = cols - (tile_start + third)
    offset = jnp.where(offset < -2, offset + total, offset)
    offset = jnp.where(offset > 0, offset - total, offset)
    return third + offset


def divided_by_3(value):
    return (value * 21846) >> 16


def diffused_terms(row, forced, center, diffuse):
    terms = [(row, 0, center[row])]
    if diffuse[row] != 0.0:
        terms += [(row, -1, -diffuse[row]), (row, 1, -diffuse[row])]
        terms += [(row + 1, 0, -diffuse[row]), (row - 1, 0, -diffuse[row])]
    return terms


def fold_times(read, write, steps):
    values = [read(t) for t in range(steps)]
    for k in range(NT):
        total = values[STEPS_PER * k]
        for gap in range(1, STEPS_PER):
            near = [values[t] for t in (STEPS_PER * k - gap, STEPS_PER * k + gap) if 0 <= t < steps]
            total = total + (1.0 - gap / STEPS_PER) * functools.reduce(jnp.add, near)
        write(k, total)


class Sizes:
    def __init__(self, cotangent_shape, tile_count):
        self.steps, self.fields, self.levels, self.forced, self.seg = cotangent_shape
        self.tiles = tile_count
        self.par = self.seg // 3
        self.total = self.par * tile_count
        self.bw = self.par // tile_count
        self.lead = NT * self.fields * self.levels
        self.group = self.levels * self.forced
        self.cols = PROWS * self.bw
        self.full = self.cols // LANES
        self.rest = self.cols % LANES
        self.share = LANES // self.rest
        self.octets = self.lead // 8
        self.rest_rows = 8 * (-(-self.octets // self.share))
        self.packed = self.full * self.lead + self.rest_rows
        self.point_tiles = self.seg // LANES


def start_fold(size, cot_ref, buffer, sems, first_tiles):
    copies = []
    for field in range(size.fields):
        for half, tile in enumerate(first_tiles):
            lanes = pl.ds(pl.multiple_of(tile * LANES, LANES), LANES)
            copy = pltpu.make_async_copy(
                cot_ref.at[:, field, :, :, lanes], buffer.at[half, field], sems.at[half, field]
            )
            copy.start()
            copies.append((half, field, copy))
    return copies


def finish_fold(size, copies, buffer, folded):
    flat = buffer.reshape(len(buffer.shape) and 2, size.fields, size.steps, size.group, LANES)
    for half, field, copy in copies:
        copy.wait()

        def read(t):
            return flat[half, field, t]

        def write(k, value):
            start = (k * size.fields + field) * size.group
            folded[half, start : start + size.group, :] = value

        fold_times(read, write, size.steps)


def block_body(size, step, me, owner_ref, cot_ref, col_ref, row_ref, along_ref, across_ref, spill_refs,
               out_ref, buffer, folded, left, right_hi, right_lo, sems):
    dest = me ^ step
    block = jnp.int32(0)
    for candidate in range(size.tiles):
        block = block + jnp.where(owner_ref[0, candidate] == dest, candidate, 0)
    first_tile = jnp.minimum(
        jnp.maximum(3 * size.bw * block - 10, 0) // LANES, size.point_tiles - 2
    )
    copies = start_fold(size, cot_ref, buffer, sems, (first_tile, first_tile + 1))

    center, diffuse = zone_factors(size.forced)
    window = 2 * LANES
    lanes = pl.ds(pl.multiple_of(first_tile * LANES, LANES), window)
    zone = col_ref.shape[0]
    lane = lax.broadcasted_iota(jnp.int32, (zone, window), 1)
    third = divided_by_3(first_tile * LANES + lane)
    first_col = first_columns(col_ref[:, lanes], third, me * size.par, size.total) - block * size.bw
    col_weights = lagrange_weights(along_ref[:, lanes])
    row_weights = lagrange_weights(across_ref[:, lanes])
    first_row = row_ref[:, lanes]

    def shifted(value, shift):
        if shift == 0:
            return value
        return pltpu.roll(value, (-shift) % window, 1)

    column = lax.broadcasted_iota(jnp.int32, (size.bw, LANES), 0)
    prow = lax.broadcasted_iota(jnp.int32, (8, LANES), 0)
    source = {}
    for shift in (-1, 0, 1):
        base = shifted(first_col, shift)
        if shift == -1:
            base = jnp.where(lane == 0, FAR, base)
        if shift == 1:
            base = jnp.where(lane == window - 1, FAR, base)
        source[shift] = (
            base,
            [shifted(w, shift) for w in col_weights],
            shifted(first_row, shift),
            [shifted(w, shift) for w in row_weights],
        )
    for half in range(2):
        part = slice(half * LANES, (half + 1) * LANES)
        tables = {}
        for row in range(size.forced):
            for zone_row, shift, _ in diffused_terms(row, size.forced, center, diffuse):
                if (zone_row, shift) in tables:
                    continue
                base, col_w, base_row, row_w = source[shift]
                one = slice(zone_row, zone_row + 1)
                tables[zone_row, shift] = (
                    tap_select(column - base[one, part], [w[one, part] for w in col_w]),
                    tap_select(prow - base_row[one, part], [w[one, part] for w in row_w]),
                )
        for row in range(size.forced):
            terms = [
                (tables[zone_row, shift][0], tables[zone_row, shift][1] * factor)
                for zone_row, shift, factor in diffused_terms(row, size.forced, center, diffuse)
            ]
            depth = slice(row * window + half * LANES, row * window + (half + 1) * LANES)
            for pair in range(PROWS // 2):
                pieces = []
                for p in (2 * pair, 2 * pair + 1):
                    products = [col_w * row_w[p : p + 1] for col_w, row_w in terms]
                    pieces.append(functools.reduce(jnp.add, products))
                high, low = split_bf16(jnp.concatenate(pieces, axis=0))
                rows = slice(2 * pair * size.bw, 2 * (pair + 1) * size.bw)
                right_hi[rows, depth] = high
                right_lo[rows, depth] = low

    if spill_refs is not None:
        left_spill, right_spill = spill_refs
        spill = jnp.concatenate(
            [left_spill[...], right_spill[...]]
            + [jnp.zeros((LANES - 2 * SPILL_ROWS, left_spill.shape[1]), jnp.float32)],
            axis=0,
        )
        across = jnp.transpose(spill)[: size.lead]
        depth = slice(size.forced * window, size.forced * window + LANES)
        high, low = split_bf16(across)
        left[: size.lead, depth] = high
        left[size.lead :, depth] = low
        column = lax.broadcasted_iota(jnp.int32, (size.cols, LANES), 0)
        entry = lax.broadcasted_iota(jnp.int32, (size.cols, LANES), 1)
        target_left = (entry >> 2) * size.bw + (entry & 3)
        right_entry = entry - SPILL_ROWS
        target_right = (right_entry >> 2) * size.bw + size.bw - SPILL + (right_entry & 3)
        hit_left = (entry < PROWS * SPILL) & (column == target_left) & (block == 0)
        hit_right = (
            (right_entry >= 0)
            & (right_entry < PROWS * SPILL)
            & (column == target_right)
            & (block == size.tiles - 1)
        )
        right_hi[:, depth] = jnp.where(hit_left | hit_right, 1.0, 0.0).astype(jnp.bfloat16)
        right_lo[:, depth] = jnp.zeros((size.cols, LANES), jnp.bfloat16)

    finish_fold(size, copies, buffer, folded)
    for half in range(2):
        for row in range(size.forced):
            high, low = split_bf16(folded[half, pl.ds(row, size.lead, stride=size.forced), :])
            depth = slice(row * window + half * LANES, row * window + (half + 1) * LANES)
            left[: size.lead, depth] = high
            left[size.lead :, depth] = low

    contract = (((1,), (1,)), ((), ()))
    top = lax.dot_general(left[...], right_hi[...], contract, preferred_element_type=jnp.float32)
    low = lax.dot_general(
        left[: size.lead], right_lo[...], contract, preferred_element_type=jnp.float32
    )
    result = top[: size.lead] + top[size.lead :] + low
    for tile in range(size.full):
        out_ref[tile * size.lead : (tile + 1) * size.lead] = result[:, tile * LANES : (tile + 1) * LANES]
    rest = result[:, size.full * LANES :]
    rest = jnp.concatenate([rest, jnp.zeros((size.lead, LANES - size.rest), jnp.float32)], axis=1)
    for octet in range(size.rest_rows // 8):
        packed = None
        for member in range(size.share):
            index = octet * size.share + member
            if index >= size.octets:
                continue
            piece = rest[8 * index : 8 * index + 8]
            if member:
                piece = pltpu.roll(piece, member * size.rest, 1)
            packed = piece if packed is None else packed + piece
        start = size.full * size.lead + 8 * octet
        out_ref[start : start + 8] = packed


def block_call(size, step, owner, cotangent, params, spills):
    with_spill = spills is not None
    depth = size.forced * 2 * LANES + (LANES if with_spill else 0)

    def kernel(*refs):
        owner_ref, me_ref, cot_ref, col_ref, row_ref, along_ref, across_ref = refs[:7]
        spill_refs = refs[7:9] if with_spill else None
        out_ref, *scratch = refs[9 if with_spill else 7 :]
        block_body(size, step, me_ref[0], owner_ref, cot_ref, col_ref, row_ref, along_ref, across_ref,
                   spill_refs, out_ref, *scratch)

    smem = pl.BlockSpec(memory_space=pltpu.SMEM)
    vmem = pl.BlockSpec(memory_space=pltpu.VMEM)
    me, *points = params
    return pl.pallas_call(
        kernel,
        out_shape=jax.ShapeDtypeStruct((size.packed, LANES), jnp.float32),
        in_specs=[smem, smem, pl.BlockSpec(memory_space=pltpu.HBM)] + [vmem] * (6 if with_spill else 4),
        out_specs=vmem,
        scratch_shapes=[
            pltpu.VMEM(
                (2, size.fields, size.steps, size.levels, size.forced, LANES), jnp.float32
            ),
            pltpu.VMEM((2, size.lead * size.forced, LANES), jnp.float32),
            pltpu.VMEM((2 * size.lead, depth), jnp.bfloat16),
            pltpu.VMEM((size.cols, depth), jnp.bfloat16),
            pltpu.VMEM((size.cols, depth), jnp.bfloat16),
            pltpu.SemaphoreType.DMA((2, size.fields)),
        ],
        compiler_params=pltpu.CompilerParams(vmem_limit_bytes=VMEM_BYTES),
        name=f"block_{step}",
    )(owner, me, cotangent, *points, *(spills or ()))


def spill_body(size, me, cot_ref, col_ref, row_ref, along_ref, across_ref, before_ref, after_ref,
               out_ref, buffer, folded, left, sems):
    last_tile = size.point_tiles - 1
    copies = start_fold(size, cot_ref, buffer, sems, (0, last_tile))
    center, diffuse = zone_factors(size.forced)
    zone = col_ref.shape[0]
    lane = lax.broadcasted_iota(jnp.int32, (zone, LANES), 1)
    entry = lax.broadcasted_iota(jnp.int32, (SPILL_ROWS, LANES), 0)
    parent_row = entry >> 2
    stencils = [[], [], [], []]
    for half, tile in enumerate((0, last_tile)):
        part = slice(tile * LANES, (tile + 1) * LANES)
        third = divided_by_3(tile * LANES + lane)
        edge_ref = before_ref if half == 0 else after_ref
        edge_lane = 0 if half == 0 else LANES - 1
        edge_shift = -1 if half == 0 else 1
        edge_third = -1 if half == 0 else size.par
        first_col = first_columns(col_ref[:, part], third, me * size.par, size.total)
        edge_tile = me * size.par
        edge_cols = edge_ref[0:zone].astype(jnp.int32)
        edge_col = first_columns(edge_cols, jnp.full_like(edge_cols, edge_third), edge_tile, size.total)
        own = [first_col, row_ref[:, part]]
        own += lagrange_weights(along_ref[:, part]) + lagrange_weights(across_ref[:, part])
        edge = [edge_col, edge_ref[8 : 8 + zone].astype(jnp.int32)]
        edge += lagrange_weights(edge_ref[16 : 16 + zone]) + lagrange_weights(edge_ref[24 : 24 + zone])
        source = {0: own}
        for shift in (-1, 1):
            moved = []
            for index, (value, other) in enumerate(zip(own, edge)):
                value = pltpu.roll(value, (-shift) % LANES, 1)
                if shift == edge_shift:
                    other = pltpu.roll(other, (-shift) % LANES, 1)
                    value = jnp.where(lane == edge_lane, other, value)
                elif index == 0:
                    value = jnp.where(lane == LANES - 1 - edge_lane, FAR, value)
                moved.append(value)
            source[shift] = moved
        edge_only = list(source[edge_shift])
        edge_only[0] = jnp.where(lane == edge_lane, edge_only[0], FAR)
        out_start = size.par if half == 1 else -SPILL
        own_start = 0 if half == 0 else size.par - SPILL

        def one(fields, row, columns):
            rows = [value[row : row + 1] for value in fields]
            along = tap_select(columns - rows[0], rows[2:6])
            across = tap_select(parent_row - rows[1], rows[6:10])
            return along * across

        for row in range(size.forced):
            terms = diffused_terms(row, size.forced, center, diffuse)
            outer = [
                one(source[shift], zone_row, (entry & 3) + out_start) * factor
                for zone_row, shift, factor in terms
            ]
            inner = [
                one(edge_only, zone_row, (entry & 3) + own_start) * factor
                for zone_row, shift, factor in terms
                if shift == edge_shift
            ] or [jnp.zeros((SPILL_ROWS, LANES), jnp.float32)]
            stencils[1 - half].append(functools.reduce(jnp.add, outer))
            stencils[2 + half].append(functools.reduce(jnp.add, inner))

    finish_fold(size, copies, buffer, folded)
    contract = (((1,), (1,)), ((), ()))
    wide = left.shape[1]
    for half in range(2):
        for row in range(size.forced):
            value = folded[half, pl.ds(row, size.lead, stride=size.forced), :]
            left[half, : size.lead, row * LANES : (row + 1) * LANES] = value
        if left.shape[1] > size.lead:
            left[half, size.lead :, :] = jnp.zeros((left.shape[1] - size.lead, left.shape[2]), jnp.float32)
    for group in range(4):
        half = 1 - group if group < 2 else group - 2
        stencil = jnp.concatenate(stencils[group], axis=1)
        out_ref[group * SPILL_ROWS : (group + 1) * SPILL_ROWS] = lax.dot_general(
            stencil, left[half], contract, precision=lax.Precision.HIGHEST,
            preferred_element_type=jnp.float32,
        )


def spill_call(size, cotangent, params, before, after):
    def kernel(me_ref, *refs):
        spill_body(size, me_ref[0], *refs)

    vmem = pl.BlockSpec(memory_space=pltpu.VMEM)
    wide = -(-size.lead // LANES) * LANES
    me, *points = params
    return pl.pallas_call(
        kernel,
        out_shape=jax.ShapeDtypeStruct((4 * SPILL_ROWS, wide), jnp.float32),
        in_specs=[pl.BlockSpec(memory_space=pltpu.SMEM), pl.BlockSpec(memory_space=pltpu.HBM)] + [vmem] * 6,
        out_specs=vmem,
        scratch_shapes=[
            pltpu.VMEM(
                (2, size.fields, size.steps, size.levels, size.forced, LANES), jnp.float32
            ),
            pltpu.VMEM((2, size.lead * size.forced, LANES), jnp.float32),
            pltpu.VMEM((2, wide, size.forced * LANES), jnp.float32),
            pltpu.SemaphoreType.DMA((2, size.fields)),
        ],
        compiler_params=pltpu.CompilerParams(vmem_limit_bytes=VMEM_BYTES),
        name="spill",
    )(me, cotangent, *points, before, after)


def place_call(size, me, arrived):
    pairs = NT * size.fields
    out_tiles = size.par // LANES

    def kernel(me_ref, *refs):
        arrived_refs, (out_ref, slots, sems) = refs[: size.tiles], refs[size.tiles :]
        copies = []
        for step in range(size.tiles):
            copy = pltpu.make_async_copy(
                arrived_refs[step], slots.at[me_ref[0] ^ step], sems.at[step]
            )
            copy.start()
            copies.append(copy)
        for copy in copies:
            copy.wait()
        lane = lax.broadcasted_iota(jnp.int32, (8, LANES), 1)

        def one_octet(index, carry):
            octet, member = index // size.share, index % size.share
            rows = [
                pl.ds(pl.multiple_of(tile * size.lead + 8 * index, 8), 8) for tile in range(size.full)
            ]
            rows.append(pl.ds(pl.multiple_of(size.full * size.lead + 8 * octet, 8), 8))
            merged = {}
            for source in range(size.tiles):
                tiles = [slots[source, r] for r in rows]
                tiles[-1] = pltpu.roll(tiles[-1], (LANES - member * size.rest) % LANES, 1)
                for p in range(PROWS):
                    done = 0
                    while done < size.bw:
                        from_lane = p * size.bw + done
                        to_lane = source * size.bw + done
                        count = min(
                            size.bw - done, LANES - from_lane % LANES, LANES - to_lane % LANES
                        )
                        value = tiles[from_lane // LANES]
                        shift = (to_lane - from_lane) % LANES
                        if shift:
                            value = pltpu.roll(value, shift, 1)
                        key = (p, to_lane // LANES)
                        start = to_lane % LANES
                        if key in merged:
                            value = jnp.where(lane >= start, value, merged[key])
                        merged[key] = value
                        done += count
            for (p, tile), value in merged.items():
                part = slice(tile * LANES, (tile + 1) * LANES)
                for k in range(8 // size.levels):
                    pair = (8 // size.levels) * index + k
                    out_ref[pair, p, :, part] = value[k * size.levels : (k + 1) * size.levels]
            return carry

        lax.fori_loop(0, size.octets, one_octet, 0)

    return pl.pallas_call(
        kernel,
        out_shape=jax.ShapeDtypeStruct((pairs, PROWS, size.levels, size.par), jnp.float32),
        in_specs=[pl.BlockSpec(memory_space=pltpu.SMEM)] + [pl.BlockSpec(memory_space=pl.ANY)] * size.tiles,
        out_specs=pl.BlockSpec(memory_space=pltpu.VMEM),
        scratch_shapes=[
            pltpu.VMEM((size.tiles, size.packed, LANES), jnp.float32),
            pltpu.SemaphoreType.DMA((size.tiles,)),
        ],
        compiler_params=pltpu.CompilerParams(vmem_limit_bytes=VMEM_BYTES),
        name="place",
    )(me, *arrived)


def edge_params(points, start):
    cols, rows, along, across = (array[:, start : start + LANES] for array in points)
    gap = jnp.zeros((8 - cols.shape[0], LANES), jnp.float32)
    parts = []
    for array in (cols.astype(jnp.float32), rows.astype(jnp.float32), along, across):
        parts += [array, gap]
    return jnp.concatenate(parts, axis=0)


def shards(cotangent, stencil_col, stencil_row, frac_along, frac_across, owner_map):
    tiles = lax.axis_size("tile")
    size = Sizes(cotangent.shape, tiles)
    me = lax.axis_index("tile").astype(jnp.int32).reshape(1)
    points = (stencil_col, stencil_row, frac_along, frac_across)
    up = [(i, (i + 1) % tiles) for i in range(tiles)]
    down = [(j, i) for i, j in up]
    before = lax.ppermute(edge_params(points, size.seg - LANES), "tile", up)
    after = lax.ppermute(edge_params(points, 0), "tile", down)
    params = (me,) + points
    spilled = spill_call(size, cotangent, params, before, after)
    group = [spilled[i * SPILL_ROWS : (i + 1) * SPILL_ROWS] for i in range(4)]
    left_spill = lax.ppermute(group[0], "tile", up) + group[2]
    right_spill = lax.ppermute(group[1], "tile", down) + group[3]
    spills = (left_spill, right_spill)
    half = tiles // 2
    order = list(range(half, tiles)) + list(range(half - 1, 0, -1))
    arrived = [None] * tiles
    for step in order:
        block = block_call(size, step, owner_map, cotangent, params, spills)
        arrived[step] = lax.ppermute(block, "tile", [(i, i ^ step) for i in range(tiles)])
    arrived[0] = block_call(size, 0, owner_map, cotangent, params, spills)
    placed = place_call(size, me, arrived)
    placed = placed.reshape(NT, size.fields, PROWS, size.levels, size.par)
    return jnp.transpose(placed, (0, 1, 3, 2, 4))


def solution(mesh):
    in_specs = (
        P(None, None, "lev", None, ("ens", "tile")),
        P(None, ("ens", "tile")),
        P(None, ("ens", "tile")),
        P(None, ("ens", "tile")),
        P(None, ("ens", "tile")),
        P(("ens", "tile"), None),
    )
    out_specs = P(None, None, "lev", None, ("ens", "tile"))
    return jax.shard_map(shards, mesh=mesh, in_specs=in_specs, out_specs=out_specs, check_vma=False)
```

```python
import functools

import jax
import jax.numpy as jnp
from jax import lax
from jax.experimental import pallas as pl
from jax.experimental.pallas import tpu as pltpu
from jax.sharding import PartitionSpec as P

PROWS = 6
NT = 12
STEPS_PER = 3
LANES = 128
TAPS = 4
SPILL = 4
SPILL_ROWS = 32
EDGE_ROWS = 40
FAR = -(1 << 20)
VMEM_BYTES = 53 << 20
BLOCK_VMEM = 32 << 20


def zone_factors(forced):
    relax = [0.0] + [(forced - r) / (forced - 1.0) for r in range(1, forced)]
    diffuse = [0.2 * value for value in relax]
    center = [1.0] + [relax[r] + 4.0 * diffuse[r] for r in range(1, forced)]
    return center, diffuse


def lagrange_weights(fraction):
    shifted = fraction + 1.0
    return [
        -fraction * (fraction - 1.0) * (fraction - 2.0) / 6.0,
        shifted * (fraction - 1.0) * (fraction - 2.0) / 2.0,
        -shifted * fraction * (fraction - 2.0) / 2.0,
        shifted * fraction * (fraction - 1.0) / 6.0,
    ]


def split_bf16(value):
    high = value.astype(jnp.bfloat16)
    low = (value - high.astype(jnp.float32)).astype(jnp.bfloat16)
    return high, low


def tap_select(distance, weights):
    picked = jnp.where(distance == TAPS - 1, weights[TAPS - 1], 0.0)
    for tap in range(TAPS - 2, -1, -1):
        picked = jnp.where(distance == tap, weights[tap], picked)
    return picked


def first_columns(cols, third, tile_start, total):
    offset = cols - (tile_start + third)
    offset = jnp.where(offset < -2, offset + total, offset)
    offset = jnp.where(offset > 0, offset - total, offset)
    return third + offset


def divided_by_3(value):
    return (value * 21846) >> 16


def diffused_terms(row, forced, center, diffuse):
    terms = [(row, 0, center[row])]
    if diffuse[row] != 0.0:
        terms += [(row, -1, -diffuse[row]), (row, 1, -diffuse[row])]
        terms += [(row + 1, 0, -diffuse[row]), (row - 1, 0, -diffuse[row])]
    return terms


def fold_times(read, write, steps):
    values = {}

    def value(t):
        if t not in values:
            values[t] = read(t)
        return values[t]

    for k in range(NT):
        total = value(STEPS_PER * k)
        for gap in range(1, STEPS_PER):
            near = [value(t) for t in (STEPS_PER * k - gap, STEPS_PER * k + gap) if 0 <= t < steps]
            total = total + (1.0 - gap / STEPS_PER) * functools.reduce(jnp.add, near)
        write(k, total)


class Sizes:
    def __init__(self, cotangent_shape, tile_count):
        self.steps, self.fields, self.levels, self.forced, self.seg = cotangent_shape
        self.tiles = tile_count
        self.par = self.seg // 3
        self.total = self.par * tile_count
        self.bw = self.par // tile_count
        self.each = NT * self.levels
        self.lead = self.fields * self.each
        self.cols = PROWS * self.bw
        self.full = self.cols // LANES
        self.rest = self.cols % LANES
        self.share = LANES // self.rest
        self.octets = self.lead // 8
        self.rest_octets = -(-self.octets // self.share)
        self.packed = self.full * self.lead + 8 * self.rest_octets
        self.point_tiles = self.seg // LANES
        self.wide = -(-self.lead // LANES) * LANES

    def fold_scratch(self, tiles):
        rows = self.levels * tiles * self.forced
        return [
            pltpu.VMEM((self.fields, self.steps, self.levels, tiles, self.forced, LANES), jnp.float32),
            pltpu.VMEM((self.fields * NT * rows, LANES), jnp.float32),
            pltpu.SemaphoreType.DMA((self.fields,)),
        ]

    def point_scratch(self, zone):
        return [
            pltpu.VMEM((2, zone, self.seg), jnp.int32),
            pltpu.VMEM((2, zone, self.seg), jnp.float32),
            pltpu.SemaphoreType.DMA((4,)),
        ]


def fold_field(size, field, tiles, buffer, folded, steps_first=False):
    rows = size.levels * tiles * size.forced
    flat = buffer.reshape(*buffer.shape[:2], rows, LANES)

    def one_part(index, carry):
        part = pl.multiple_of(16 * index, 16)

        def write(k, value):
            start = (field * NT + k) * rows
            folded[pl.ds(start + part, 16), :] = value

        fold_times(
            lambda t: flat[t, field, pl.ds(part, 16)] if steps_first else flat[field, t, pl.ds(part, 16)],
            write,
            size.steps,
        )
        return carry

    lax.fori_loop(0, rows // 16, one_part, 0)


def folded_rows(size, folded, first_field, count, tiles, tile, row):
    rows = size.levels * tiles * size.forced
    start = first_field * NT * rows + tile * size.forced + row
    return folded[pl.ds(start, count * size.each, stride=tiles * size.forced), :]


def start_points(point_refs, ints, floats, sems):
    copies = []
    for index, ref in enumerate(point_refs):
        target = (ints if index < 2 else floats).at[index % 2]
        copy = pltpu.make_async_copy(ref, target, sems.at[index])
        copy.start()
        copies.append(copy)
    return copies


def block_stencil(size, me, block, first_tile, ints, floats, right_hi, right_lo):
    center, diffuse = zone_factors(size.forced)
    window = 2 * LANES
    lanes = pl.ds(pl.multiple_of(first_tile * LANES, LANES), window)
    zone = ints.shape[1]
    lane = lax.broadcasted_iota(jnp.int32, (zone, window), 1)
    third = divided_by_3(first_tile * LANES + lane)
    first_col = first_columns(ints[0, :, lanes], third, me * size.par, size.total) - block * size.bw
    col_weights = lagrange_weights(floats[0, :, lanes])
    row_weights = lagrange_weights(floats[1, :, lanes])
    first_row = ints[1, :, lanes]

    def shifted(value, shift):
        if shift == 0:
            return value
        return pltpu.roll(value, (-shift) % window, 1)

    column = lax.broadcasted_iota(jnp.int32, (size.bw, LANES), 0)
    prow = lax.broadcasted_iota(jnp.int32, (8, LANES), 0)
    source = {}
    for shift in (-1, 0, 1):
        base = shifted(first_col, shift)
        if shift == -1:
            base = jnp.where(lane == 0, FAR, base)
        if shift == 1:
            base = jnp.where(lane == window - 1, FAR, base)
        source[shift] = (
            base,
            [shifted(w, shift) for w in col_weights],
            shifted(first_row, shift),
            [shifted(w, shift) for w in row_weights],
        )
    for half in range(2):
        part = slice(half * LANES, (half + 1) * LANES)
        tables = {}
        for row in range(size.forced):
            for zone_row, shift, _ in diffused_terms(row, size.forced, center, diffuse):
                if (zone_row, shift) in tables:
                    continue
                base, col_w, base_row, row_w = source[shift]
                one = slice(zone_row, zone_row + 1)
                tables[zone_row, shift] = (
                    tap_select(column - base[one, part], [w[one, part] for w in col_w]),
                    tap_select(prow - base_row[one, part], [w[one, part] for w in row_w]),
                )
        for row in range(size.forced):
            terms = [
                (tables[zone_row, shift][0], tables[zone_row, shift][1] * factor)
                for zone_row, shift, factor in diffused_terms(row, size.forced, center, diffuse)
            ]
            depth = slice(row * window + half * LANES, row * window + (half + 1) * LANES)
            for pair in range(PROWS // 2):
                pieces = []
                for p in (2 * pair, 2 * pair + 1):
                    products = [col_w * row_w[p : p + 1] for col_w, row_w in terms]
                    pieces.append(functools.reduce(jnp.add, products))
                high, low = split_bf16(jnp.concatenate(pieces, axis=0))
                rows = slice(2 * pair * size.bw, 2 * (pair + 1) * size.bw)
                right_hi[rows, depth] = high
                right_lo[rows, depth] = low


def spill_hits(size, entry, column, at_left, at_right):
    side = (entry // SPILL_ROWS) & 1
    inner = entry & (SPILL_ROWS - 1)
    target = (inner >> 2) * size.bw + (inner & 3)
    on_left = (side == 0) & at_left & (column == target)
    on_right = (side == 1) & at_right & (column == target + size.bw - SPILL)
    return jnp.where((inner < PROWS * SPILL) & (on_left | on_right), 1.0, 0.0).astype(jnp.bfloat16)


def block_of(size, owner_ref, dest):
    block = jnp.int32(0)
    for candidate in range(size.tiles):
        block = block + jnp.where(owner_ref[0, candidate] == dest, candidate, 0)
    return block


def pack_rest(size, rest, out_ref):
    rest = jnp.concatenate([rest, jnp.zeros((size.lead, LANES - size.rest), jnp.float32)], axis=1)
    for octet in range(size.rest_octets):
        packed = None
        for member in range(size.share):
            index = member * size.rest_octets + octet
            if index >= size.octets:
                continue
            piece = rest[8 * index : 8 * index + 8]
            if member:
                piece = pltpu.roll(piece, member * size.rest, 1)
            packed = piece if packed is None else packed + piece
        start = size.full * size.lead + 8 * octet
        out_ref[start : start + 8] = packed


def product(left, right_hi, right_lo):
    contract = (((1,), (1,)), ((), ()))
    count = left.shape[0] // 2
    both = lax.dot_general(left, right_hi, contract, preferred_element_type=jnp.float32)
    extra = lax.dot_general(left[:count], right_lo, contract, preferred_element_type=jnp.float32)
    return both[:count] + both[count:] + extra


def window_of(size, block):
    first = jnp.maximum(3 * size.bw * block - 10, 0) // LANES
    return jnp.minimum(first, size.point_tiles - 2)


def first_call(size, step, owner, cotangent, points):
    zone = points[0].shape[0]
    window = 2 * LANES
    depth = size.forced * window
    chunks = ((0, size.fields - 2), (size.fields - 2, size.fields))

    def kernel(owner_hbm, cot_ref, *refs):
        point_refs, out_ref, edge_refs, refs = refs[:4], refs[4], refs[5:7], refs[7:]
        owner_ref, owner_sem, buffer, folded, sems, ints, floats, point_sems, left, right_hi, right_lo = refs[:-3]
        edge_buffer, edge_folded, edge_sems = refs[-3:]
        owner_copy = pltpu.make_async_copy(owner_hbm, owner_ref, owner_sem)
        owner_copy.start()
        point_copies = start_points(point_refs, ints, floats, point_sems)
        edge_copies = []
        for end, tile in enumerate((0, size.point_tiles - 1)):
            copy = pltpu.make_async_copy(
                cot_ref.at[:, :, :, pl.ds(tile, 1)], edge_buffer.at[:, :, :, pl.ds(end, 1)], edge_sems.at[end]
            )
            copy.start()
            edge_copies.append(copy)
        me = lax.axis_index("tile")
        owner_copy.wait()
        block = block_of(size, owner_ref, me ^ step)
        first_tile = window_of(size, block)
        copies = []
        for field in range(size.fields):
            copy = pltpu.make_async_copy(
                cot_ref.at[:, field, :, pl.ds(first_tile, 2)], buffer.at[field], sems.at[field]
            )
            copy.start()
            copies.append(copy)
        for copy in point_copies:
            copy.wait()
        center, diffuse = zone_factors(size.forced)
        lane = lax.broadcasted_iota(jnp.int32, (zone, LANES), 1)
        entry = lax.broadcasted_iota(jnp.int32, (SPILL_ROWS, LANES), 0)
        entry_lane = lax.broadcasted_iota(jnp.int32, (SPILL_ROWS, LANES), 1)
        parent_row = entry >> 2
        stencils = []
        for tile, edge_lane, out_start in ((0, 0, -SPILL), (size.point_tiles - 1, LANES - 1, size.par)):
            part = slice(tile * LANES, (tile + 1) * LANES)
            third = divided_by_3(tile * LANES + lane)
            first_col = first_columns(ints[0, :, part], third, me * size.par, size.total)
            own = [first_col, ints[1, :, part]]
            own += lagrange_weights(floats[0, :, part]) + lagrange_weights(floats[1, :, part])
            source = {0: own}
            for shift in (-1, 1):
                moved = [pltpu.roll(value, (-shift) % LANES, 1) for value in own]
                moved[0] = jnp.where(lane == (0 if shift == -1 else LANES - 1), FAR, moved[0])
                source[shift] = moved

            def one(values, row):
                rows = [value[row : row + 1] for value in values]
                along = tap_select((entry & 3) + out_start - rows[0], rows[2:6])
                across = tap_select(parent_row - rows[1], rows[6:10])
                return along * across

            stencil = []
            for row in range(size.forced):
                terms = [
                    one(source[shift], zone_row) * factor
                    for zone_row, shift, factor in diffused_terms(row, size.forced, center, diffuse)
                ]
                picks = (entry == PROWS * SPILL + row - 1) & (entry_lane == edge_lane) & (row > 0)
                stencil.append(jnp.where(picks, 1.0, functools.reduce(jnp.add, terms)))
            stencils.append(jnp.concatenate(stencil, axis=1))

        for copy in edge_copies:
            copy.wait()
        for field in range(size.fields):
            fold_field(size, field, 2, edge_buffer, edge_folded, steps_first=True)
        contract = (((1,), (1,)), ((), ()))
        for end in range(2):
            parts = []
            for row in range(size.forced):
                values = folded_rows(size, edge_folded, 0, size.fields, 2, end, row)
                parts.append(jnp.concatenate(split_bf16(values), axis=0))
            right = jnp.concatenate(parts, axis=1)
            high, low = split_bf16(stencils[end])
            both = lax.dot_general(high, right, contract, preferred_element_type=jnp.float32)
            extra = lax.dot_general(low, right[: size.lead], contract, preferred_element_type=jnp.float32)
            edge_ref = edge_refs[end]
            edge_ref[...] = jnp.zeros((EDGE_ROWS, size.wide), jnp.float32)
            edge_ref[:SPILL_ROWS, : size.lead] = both[:, : size.lead] + both[:, size.lead :] + extra
            point = 0 if end == 0 else size.seg - 1
            start = PROWS * SPILL + size.forced - 1
            for kind in range(4):
                for row in range(1, size.forced):
                    value = (ints if kind < 2 else floats)[kind % 2, row : row + 1, point : point + 1]
                    edge_ref[start : start + 1] = jnp.broadcast_to(value.astype(jnp.float32), (1, size.wide))
                    start += 1
        block_stencil(size, me, block, first_tile, ints, floats, right_hi, right_lo)
        pieces = []
        for first, last in chunks:
            for field in range(first, last):
                copies[field].wait()
                fold_field(size, field, 2, buffer, folded)
            base, count = 2 * first * size.each, (last - first) * size.each
            for half in range(2):
                for row in range(size.forced):
                    high, low = split_bf16(folded_rows(size, folded, first, last - first, 2, half, row))
                    part = slice(row * window + half * LANES, row * window + (half + 1) * LANES)
                    left[base : base + count, part] = high
                    left[base + count : base + 2 * count, part] = low
            result = product(left[base : base + 2 * count], right_hi[...], right_lo[...])
            for tile in range(size.full):
                start = tile * size.lead + first * size.each
                out_ref[start : start + count] = result[:, tile * LANES : (tile + 1) * LANES]
            pieces.append(result[:, size.full * LANES :])
        pack_rest(size, jnp.concatenate(pieces, axis=0), out_ref)

    vmem = pl.BlockSpec(memory_space=pltpu.VMEM)
    hbm = pl.BlockSpec(memory_space=pltpu.HBM)
    return pl.pallas_call(
        kernel,
        out_shape=[pltpu.VMEM((size.packed, LANES), jnp.float32)]
        + [pltpu.VMEM((EDGE_ROWS, size.wide), jnp.float32)] * 2,
        in_specs=[hbm] * 6,
        out_specs=[vmem] * 3,
        scratch_shapes=[pltpu.SMEM((1, size.tiles), jnp.int32), pltpu.SemaphoreType.DMA]
        + size.fold_scratch(2)
        + size.point_scratch(zone)
        + [
            pltpu.VMEM((2 * size.lead, depth), jnp.bfloat16),
            pltpu.VMEM((size.cols, depth), jnp.bfloat16),
            pltpu.VMEM((size.cols, depth), jnp.bfloat16),
            pltpu.VMEM((size.steps, size.fields, size.levels, 2, size.forced, LANES), jnp.float32),
            pltpu.VMEM((size.lead * 2 * size.forced, LANES), jnp.float32),
            pltpu.SemaphoreType.DMA((2,)),
        ],
        compiler_params=pltpu.CompilerParams(vmem_limit_bytes=VMEM_BYTES),
        name=f"block_{step}",
    )(in_hbm(owner), in_hbm(cotangent), *map(in_hbm, points))


def write_blocks(size, steps, owner_ref, parts_ref, ints, floats, across_ref, out_refs, right_hi, right_lo):
    inner = size.forced * 2 * LANES
    me = lax.axis_index("tile")
    for step, out_ref in zip(steps, out_refs):
        block = block_of(size, owner_ref, me ^ step)
        first_tile = window_of(size, block)
        block_stencil(size, me, block, first_tile, ints, floats, right_hi, right_lo)
        left = [
            parts_ref[first_tile + half, row] for row in range(size.forced) for half in range(2)
        ]
        left.append(across_ref[...])
        column = lax.broadcasted_iota(jnp.int32, (size.cols, LANES), 0)
        entry = lax.broadcasted_iota(jnp.int32, (size.cols, LANES), 1)
        right_hi[:, inner:] = spill_hits(size, entry, column, block == 0, block == size.tiles - 1)
        right_lo[:, inner:] = jnp.zeros((size.cols, LANES), jnp.bfloat16)
        result = product(jnp.concatenate(left, axis=1), right_hi[...], right_lo[...])
        for tile in range(size.full):
            start = tile * size.lead
            out_ref[start : start + size.lead] = result[:, tile * LANES : (tile + 1) * LANES]
        pack_rest(size, result[:, size.full * LANES :], out_ref)


def block_call(size, steps, owner, parts, ints, floats, across, fix=None, after=(), unread=()):
    depth = size.forced * 2 * LANES + LANES

    def kernel(owner_ref, parts_ref, ints, floats, across_ref, *refs):
        if fix is not None:
            fix_ref, refs = refs[0], refs[1:]
        refs = refs[len(after) + len(unread) :]
        out_refs, refs = refs[: len(steps)], refs[len(steps) :]
        if fix is not None:
            refs[0][...] = fix_ref[...]
            refs = refs[1:]
        right_hi, right_lo = refs
        write_blocks(size, steps, owner_ref, parts_ref, ints, floats, across_ref, out_refs, right_hi, right_lo)

    vmem = pl.BlockSpec(memory_space=pltpu.VMEM)
    operands = [parts, ints, floats, across] + ([] if fix is None else [fix]) + list(after)
    outs = [pltpu.VMEM((size.packed, LANES), jnp.float32)] * len(steps)
    if fix is not None:
        outs.append(pltpu.VMEM((SPILL_ROWS, size.wide), jnp.float32))
    return pl.pallas_call(
        kernel,
        out_shape=outs,
        in_specs=[pl.BlockSpec(memory_space=pltpu.SMEM)]
        + [vmem] * len(operands)
        + [pl.BlockSpec(memory_space=pltpu.HBM)] * len(unread),
        out_specs=[vmem] * len(outs),
        scratch_shapes=[pltpu.VMEM((size.cols, depth), jnp.bfloat16)] * 2,
        compiler_params=pltpu.CompilerParams(vmem_limit_bytes=BLOCK_VMEM),
        name="block_" + "_".join(map(str, steps)),
    )(owner, *map(in_vmem, operands), *map(in_hbm, unread))


def in_vmem(array):
    return pltpu.with_memory_space_constraint(array, pltpu.VMEM)


def in_hbm(array):
    return pltpu.with_memory_space_constraint(array, pltpu.HBM)


def fold_call(size, cotangent, points, after):
    zone = points[0].shape[0]

    def kernel(cot_ref, *refs):
        point_refs, parts_ref, ints, floats, buffer, folded, sems, point_sems = refs[:4], *refs[4 + len(after) :]
        point_copies = start_points(point_refs, ints, floats, point_sems)
        copies = []
        for field in range(size.fields):
            copy = pltpu.make_async_copy(cot_ref.at[:, field], buffer.at[field], sems.at[field])
            copy.start()
            copies.append(copy)
        for copy in point_copies:
            copy.wait()
        for field in range(size.fields):
            copies[field].wait()
            fold_field(size, field, size.point_tiles, buffer, folded)
            rows = slice(field * size.each, (field + 1) * size.each)
            low_rows = slice(size.lead + field * size.each, size.lead + (field + 1) * size.each)
            for tile in range(size.point_tiles):
                for row in range(size.forced):
                    values = folded_rows(size, folded, field, 1, size.point_tiles, tile, row)
                    parts_ref[tile, row, rows], parts_ref[tile, row, low_rows] = split_bf16(values)

    vmem = pl.BlockSpec(memory_space=pltpu.VMEM)
    hbm = pl.BlockSpec(memory_space=pltpu.HBM)
    return pl.pallas_call(
        kernel,
        out_shape=[
            pltpu.VMEM((size.point_tiles, size.forced, 2 * size.lead, LANES), jnp.bfloat16),
            pltpu.VMEM((2, zone, size.seg), jnp.int32),
            pltpu.VMEM((2, zone, size.seg), jnp.float32),
        ],
        in_specs=[hbm] * 5 + [vmem] * len(after),
        out_specs=[vmem] * 3,
        scratch_shapes=size.fold_scratch(size.point_tiles) + size.point_scratch(zone)[2:],
        compiler_params=pltpu.CompilerParams(vmem_limit_bytes=VMEM_BYTES),
        name="fold",
    )(in_hbm(cotangent), *map(in_hbm, points), *map(in_vmem, after))


def join_call(size, early, step, owner, edges, from_left, from_right, parts, ints, floats):
    depth = size.forced * 2 * LANES + LANES

    def kernel(owner_ref, *refs):
        left_ref, right_ref, from_left_ref, from_right_ref, parts_ref, ints, floats = refs[:7]
        across_ref, fix_ref, out_ref, right_hi, right_lo = refs[7:]
        me = lax.axis_index("tile")
        _, diffuse = zone_factors(size.forced)
        entry = lax.broadcasted_iota(jnp.int32, (SPILL_ROWS, size.wide), 0)
        spills = []
        for own_ref, other_ref, own_point, other_third, first in (
            (left_ref, from_left_ref, 0, -1, 0),
            (right_ref, from_right_ref, size.seg - 1, size.par, size.par - SPILL),
        ):
            total = other_ref[:SPILL_ROWS]
            column = (entry & 3) + first
            for row in range(1, size.forced):
                start = PROWS * SPILL + size.forced - 1

                def stencil(ref, third):
                    kinds = [
                        ref[start + kind * (size.forced - 1) + row - 1 :][:1] for kind in range(4)
                    ]
                    cols = kinds[0].astype(jnp.int32)
                    base = first_columns(cols, jnp.full_like(cols, third), me * size.par, size.total)
                    along = tap_select(column - base, lagrange_weights(kinds[2]))
                    across = tap_select((entry >> 2) - kinds[1].astype(jnp.int32), lagrange_weights(kinds[3]))
                    return along * across

                folded_row = PROWS * SPILL + row - 1
                here = stencil(own_ref, own_point // 3) * other_ref[folded_row : folded_row + 1]
                there = stencil(other_ref, other_third) * own_ref[folded_row : folded_row + 1]
                total = total - diffuse[row] * (here + there)
            spills.append(jnp.where(entry < PROWS * SPILL, total, 0.0))
        blank = jnp.zeros((LANES - 2 * SPILL_ROWS, size.wide), jnp.float32)
        across = jnp.transpose(jnp.concatenate(spills + [blank], axis=0))[: size.lead]
        across_ref[: size.lead], across_ref[size.lead :] = split_bf16(across)
        fixed = block_of(size, owner_ref, me ^ early)
        fix = jnp.where(fixed == 0, spills[0], jnp.where(fixed == size.tiles - 1, spills[1], 0.0))
        flag = jnp.where(fixed == 0, 1.0, 0.0)
        fix_ref[...] = jnp.where(entry == SPILL_ROWS - 1, flag, fix)
        write_blocks(
            size, [step], owner_ref, parts_ref, ints, floats, across_ref, [out_ref], right_hi, right_lo
        )

    vmem = pl.BlockSpec(memory_space=pltpu.VMEM)
    return pl.pallas_call(
        kernel,
        out_shape=[
            pltpu.VMEM((2 * size.lead, LANES), jnp.bfloat16),
            pltpu.VMEM((SPILL_ROWS, size.wide), jnp.float32),
            pltpu.VMEM((size.packed, LANES), jnp.float32),
        ],
        in_specs=[pl.BlockSpec(memory_space=pltpu.SMEM)] + [vmem] * 7,
        out_specs=[vmem] * 3,
        scratch_shapes=[pltpu.VMEM((size.cols, depth), jnp.bfloat16)] * 2,
        compiler_params=pltpu.CompilerParams(vmem_limit_bytes=BLOCK_VMEM),
        name="join",
    )(owner, *map(in_vmem, [*edges, from_left, from_right, parts, ints, floats]))


def fix_call(size, block, fix):
    def kernel(block_ref, fix_ref, out_ref):
        values = fix_ref[...]
        values = jnp.concatenate(
            [values, jnp.zeros((LANES - SPILL_ROWS, size.wide), jnp.float32)], axis=0
        )
        across = jnp.transpose(values)[: size.lead]
        at_left = fix_ref[SPILL_ROWS - 1, 0] > 0.5
        column = lax.broadcasted_iota(jnp.int32, (size.cols, LANES), 0)
        entry = lax.broadcasted_iota(jnp.int32, (size.cols, LANES), 1)
        hits = [
            spill_hits(size, entry + SPILL_ROWS * side, column, side == 0, side == 1) for side in range(2)
        ]
        inside = entry < SPILL_ROWS
        right = jnp.where(at_left, hits[0].astype(jnp.float32), hits[1].astype(jnp.float32))
        right = jnp.where(inside, right, 0.0).astype(jnp.bfloat16)
        high, low = split_bf16(across)
        contract = (((1,), (1,)), ((), ()))
        both = lax.dot_general(
            jnp.concatenate([high, low], axis=0), right, contract, preferred_element_type=jnp.float32
        )
        result = both[: size.lead] + both[size.lead :]
        for tile in range(size.full):
            rows = slice(tile * size.lead, (tile + 1) * size.lead)
            out_ref[rows] = block_ref[rows] + result[:, tile * LANES : (tile + 1) * LANES]
        rows = slice(size.full * size.lead, size.packed)
        pack_rest(size, result[:, size.full * LANES :], out_ref)
        out_ref[rows] += block_ref[rows]

    vmem = pl.BlockSpec(memory_space=pltpu.VMEM)
    return pl.pallas_call(
        kernel,
        out_shape=pltpu.VMEM((size.packed, LANES), jnp.float32),
        in_specs=[vmem] * 2,
        out_specs=vmem,
        compiler_params=pltpu.CompilerParams(vmem_limit_bytes=VMEM_BYTES),
        name="fix",
    )(in_vmem(block), in_vmem(fix))


def pieces(size, source, member):
    for p in range(PROWS):
        done = 0
        while done < size.bw:
            from_lane = p * size.bw + done
            to_lane = source * size.bw + done
            count = min(size.bw - done, LANES - from_lane % LANES, LANES - to_lane % LANES)
            held = from_lane // LANES
            extra = member * size.rest if held == size.full else 0
            start = to_lane % LANES
            yield p, to_lane // LANES, start, start + count, held, (to_lane - from_lane - extra) % LANES
            done += count


def each_octet(size, one_octet):
    def body(i, carry):
        for member in range(size.share):
            octet = member * size.rest_octets + i
            if (member + 1) * size.rest_octets <= size.octets:
                one_octet(octet, member)
            else:
                pl.when(octet < size.octets)(functools.partial(one_octet, octet, member))
        return carry

    lax.fori_loop(0, size.rest_octets, body, 0)


def octet_rows(size, octet, member):
    rows = [pl.ds(pl.multiple_of(tile * size.lead + 8 * octet, 8), 8) for tile in range(size.full)]
    start = size.full * size.lead + 8 * (octet - member * size.rest_octets)
    return rows + [pl.ds(pl.multiple_of(start, 8), 8)]


def octet_pairs(size, octet):
    per_octet = 8 // size.levels
    field = octet // (NT // per_octet)
    time = per_octet * (octet - field * (NT // per_octet))
    return [(time + k) * size.fields + field for k in range(per_octet)]


def merge(size, refs, position, octet, member, merged):
    lane = lax.broadcasted_iota(jnp.int32, (8, LANES), 1)
    rows = octet_rows(size, octet, member)
    for source in range(size.tiles):
        if source ^ position not in refs:
            continue
        tiles = [refs[source ^ position][r] for r in rows]
        for p, tile, start, stop, held, shift in pieces(size, source, member):
            value = pltpu.roll(tiles[held], shift, 1) if shift else tiles[held]
            if (p, tile) in merged:
                value = jnp.where((lane >= start) & (lane < stop), value, merged[p, tile])
            merged[p, tile] = value


def at_position(size, one_octet):
    me = lax.axis_index("tile")
    for position in range(size.tiles):
        pl.when(me == position)(functools.partial(each_octet, size, functools.partial(one_octet, position)))


def place_call(size, arrived, unread):
    shape = (size.octets, PROWS, size.par // LANES, 8, LANES)

    def kernel(*refs):
        blocks, staged = dict(zip(arrived, refs)), refs[-1]

        def one_octet(position, octet, member):
            merged = {}
            merge(size, blocks, position, octet, member, merged)
            for (p, tile), value in merged.items():
                staged[octet, p, tile] = value

        at_position(size, one_octet)

    vmem = pl.BlockSpec(memory_space=pltpu.VMEM)
    return pl.pallas_call(
        kernel,
        out_shape=pltpu.VMEM(shape, jnp.float32),
        in_specs=[vmem] * len(arrived) + [pl.BlockSpec(memory_space=pltpu.HBM)],
        out_specs=vmem,
        compiler_params=pltpu.CompilerParams(vmem_limit_bytes=BLOCK_VMEM),
        name="place",
    )(*map(in_vmem, arrived.values()), in_hbm(unread))


def finish_call(size, staged, arrived):
    shape = (NT * size.fields, PROWS, size.levels, size.par)

    def kernel(staged_ref, *refs):
        blocks, (out_ref, final, sem) = dict(zip(arrived, refs)), refs[len(arrived) :]

        def one_octet(position, octet, member):
            merged = {
                (p, tile): staged_ref[octet, p, tile]
                for p in range(PROWS)
                for tile in range(size.par // LANES)
            }
            merge(size, blocks, position, octet, member, merged)
            for k, pair in enumerate(octet_pairs(size, octet)):
                for (p, tile), value in merged.items():
                    part = slice(tile * LANES, (tile + 1) * LANES)
                    final[pair, p, :, part] = value[k * size.levels : (k + 1) * size.levels]
                pltpu.make_async_copy(final.at[pair], out_ref.at[pair], sem).start()

        at_position(size, one_octet)
        pltpu.make_async_copy(final, out_ref, sem).wait()

    vmem = pl.BlockSpec(memory_space=pltpu.VMEM)
    return pl.pallas_call(
        kernel,
        out_shape=jax.ShapeDtypeStruct(shape, jnp.float32),
        in_specs=[vmem] * (1 + len(arrived)),
        out_specs=pl.BlockSpec(memory_space=pltpu.HBM),
        scratch_shapes=[pltpu.VMEM(shape, jnp.float32), pltpu.SemaphoreType.DMA],
        compiler_params=pltpu.CompilerParams(vmem_limit_bytes=BLOCK_VMEM),
        name="finish",
    )(in_vmem(staged), *map(in_vmem, arrived.values()))


def more_call(size, staged, arrived, unread):
    shape = staged.shape

    def kernel(*refs):
        blocks, staged_ref = dict(zip(arrived, refs[1:])), refs[-1]

        def one_octet(position, octet, member):
            touched = {
                source ^ position: [
                    (p, tile) for p, tile, *_ in pieces(size, source, member)
                ]
                for source in range(size.tiles)
                if source ^ position in blocks
            }
            merged = {
                (p, tile): staged_ref[octet, p, tile] for keys in touched.values() for p, tile in keys
            }
            merge(size, blocks, position, octet, member, merged)
            for (p, tile), value in merged.items():
                staged_ref[octet, p, tile] = value

        at_position(size, one_octet)

    vmem = pl.BlockSpec(memory_space=pltpu.VMEM)
    return pl.pallas_call(
        kernel,
        out_shape=pltpu.VMEM(shape, jnp.float32),
        in_specs=[vmem] * (1 + len(arrived)) + [pl.BlockSpec(memory_space=pltpu.HBM)],
        out_specs=vmem,
        input_output_aliases={0: 0},
        compiler_params=pltpu.CompilerParams(vmem_limit_bytes=BLOCK_VMEM),
        name="more",
    )(in_vmem(staged), *map(in_vmem, arrived.values()), in_hbm(unread))


def shards(cotangent, stencil_col, stencil_row, frac_along, frac_across, owner_map):
    tiles = lax.axis_size("tile")
    size = Sizes(cotangent.shape, tiles)
    points = (stencil_col, stencil_row, frac_along, frac_across)
    up = [(i, (i + 1) % tiles) for i in range(tiles)]
    down = [(j, i) for i, j in up]
    tiled = cotangent.reshape(cotangent.shape[:-1] + (size.point_tiles, LANES))
    tiled = jnp.transpose(tiled, (0, 1, 2, 4, 3, 5))
    half = tiles // 2
    far, near = list(range(half, tiles)), list(range(half - 1, 0, -1))
    arrived = [None] * tiles

    def send(step, value):
        return lax.ppermute(value, "tile", [(i, i ^ step) for i in range(tiles)])

    early = far[0]
    first, *edges = first_call(size, early, owner_map, tiled, points)
    arrived[early] = send(early, first)
    from_right = lax.ppermute(edges[0], "tile", down)
    from_left = lax.ppermute(edges[1], "tile", up)
    parts, ints, floats = fold_call(size, tiled, points, edges)
    across, fix, block = join_call(
        size, early, far[1], owner_map, edges, from_left, from_right, parts, ints, floats
    )
    arrived[far[1]] = send(far[1], block)
    made = [block]
    turns = [kind[i : i + 2] for kind in (far[2:], near) for i in range(0, len(kind), 2)]
    for turn in turns:
        fixes = turn[0] == near[0]
        after = list(made[:1]) + ([arrived[early]] if fixes else [])
        made = block_call(size, turn, owner_map, parts, ints, floats, across, fix if fixes else None, after)
        for step, block in zip(turn, made):
            arrived[step] = send(step, block)
        if fixes:
            fix = send(early, made[-1])
    arrived[0] = block_call(size, [0], owner_map, parts, ints, floats, across)[0]
    arrived[early] = fix_call(size, arrived[early], fix)
    staged = place_call(size, {step: arrived[step] for step in (far[1], early, 0)}, tiled)
    for turn in turns[:-1]:
        staged = more_call(size, staged, {step: arrived[step] for step in turn}, tiled)
    placed = finish_call(size, staged, {step: arrived[step] for step in turns[-1]})
    placed = placed.reshape(NT, size.fields, PROWS, size.levels, size.par)
    return jnp.transpose(placed, (0, 1, 3, 2, 4))


def solution(mesh):
    in_specs = (
        P(None, None, "lev", None, ("ens", "tile")),
        P(None, ("ens", "tile")),
        P(None, ("ens", "tile")),
        P(None, ("ens", "tile")),
        P(None, ("ens", "tile")),
        P(("ens", "tile"), None),
    )
    out_specs = P(None, None, "lev", None, ("ens", "tile"))
    return jax.shard_map(shards, mesh=mesh, in_specs=in_specs, out_specs=out_specs, check_vma=False)
```

```python
import functools

import jax
import jax.numpy as jnp
from jax import lax
from jax.experimental import pallas as pl
from jax.experimental.pallas import tpu as pltpu
from jax.sharding import PartitionSpec as P

PROWS = 6
NT = 12
STEPS_PER = 3
LANES = 128
TAPS = 4
SPILL = 4
SPILL_ROWS = 32
EDGE_ROWS = 40
FAR = -(1 << 20)
VMEM_BYTES = 28 << 20
BLOCK_VMEM = 16 << 20


def zone_factors(forced):
    relax = [0.0] + [(forced - r) / (forced - 1.0) for r in range(1, forced)]
    diffuse = [0.2 * value for value in relax]
    center = [1.0] + [relax[r] + 4.0 * diffuse[r] for r in range(1, forced)]
    return center, diffuse


def lagrange_weights(fraction):
    shifted = fraction + 1.0
    return [
        -fraction * (fraction - 1.0) * (fraction - 2.0) / 6.0,
        shifted * (fraction - 1.0) * (fraction - 2.0) / 2.0,
        -shifted * fraction * (fraction - 2.0) / 2.0,
        shifted * fraction * (fraction - 1.0) / 6.0,
    ]


def split_bf16(value):
    high = value.astype(jnp.bfloat16)
    low = (value - high.astype(jnp.float32)).astype(jnp.bfloat16)
    return high, low


def tap_select(distance, weights):
    picked = jnp.where(distance == TAPS - 1, weights[TAPS - 1], 0.0)
    for tap in range(TAPS - 2, -1, -1):
        picked = jnp.where(distance == tap, weights[tap], picked)
    return picked


def first_columns(cols, third, tile_start, total):
    offset = cols - (tile_start + third)
    offset = jnp.where(offset < -2, offset + total, offset)
    offset = jnp.where(offset > 0, offset - total, offset)
    return third + offset


def divided_by_3(value):
    return (value * 21846) >> 16


def diffused_terms(row, forced, center, diffuse):
    terms = [(row, 0, center[row])]
    if diffuse[row] != 0.0:
        terms += [(row, -1, -diffuse[row]), (row, 1, -diffuse[row])]
        terms += [(row + 1, 0, -diffuse[row]), (row - 1, 0, -diffuse[row])]
    return terms


def fold_times(read, write, steps):
    values = {}

    def value(t):
        if t not in values:
            values[t] = read(t)
        return values[t]

    for k in range(NT):
        total = value(STEPS_PER * k)
        for gap in range(1, STEPS_PER):
            near = [value(t) for t in (STEPS_PER * k - gap, STEPS_PER * k + gap) if 0 <= t < steps]
            total = total + (1.0 - gap / STEPS_PER) * functools.reduce(jnp.add, near)
        write(k, total)


class Sizes:
    def __init__(self, cotangent_shape, tile_count):
        self.steps, self.fields, self.levels, self.forced, self.seg = cotangent_shape
        self.tiles = tile_count
        self.par = self.seg // 3
        self.total = self.par * tile_count
        self.bw = self.par // tile_count
        self.each = NT * self.levels
        self.lead = self.fields * self.each
        self.cols = PROWS * self.bw
        self.full = self.cols // LANES
        self.rest = self.cols % LANES
        self.share = LANES // self.rest
        self.octets = self.lead // 8
        self.rest_octets = -(-self.octets // self.share)
        self.packed = self.full * self.lead + 8 * self.rest_octets
        self.point_tiles = self.seg // LANES
        self.wide = -(-self.lead // LANES) * LANES

    def fold_scratch(self, tiles):
        rows = self.levels * tiles * self.forced
        return [
            pltpu.VMEM((self.fields, self.steps, self.levels, tiles, self.forced, LANES), jnp.float32),
            pltpu.VMEM((self.fields * NT * rows, LANES), jnp.float32),
            pltpu.SemaphoreType.DMA((self.fields,)),
        ]

    def point_scratch(self, zone):
        return [
            pltpu.VMEM((2, zone, self.seg), jnp.int32),
            pltpu.VMEM((2, zone, self.seg), jnp.float32),
            pltpu.SemaphoreType.DMA((4,)),
        ]


def fold_field(size, field, tiles, buffer, folded, steps_first=False):
    rows = size.levels * tiles * size.forced
    flat = buffer.reshape(*buffer.shape[:2], rows, LANES)

    def one_part(index, carry):
        part = pl.multiple_of(16 * index, 16)

        def write(k, value):
            start = (field * NT + k) * rows
            folded[pl.ds(start + part, 16), :] = value

        fold_times(
            lambda t: flat[t, field, pl.ds(part, 16)] if steps_first else flat[field, t, pl.ds(part, 16)],
            write,
            size.steps,
        )
        return carry

    lax.fori_loop(0, rows // 16, one_part, 0)


def folded_rows(size, folded, first_field, count, tiles, tile, row):
    rows = size.levels * tiles * size.forced
    start = first_field * NT * rows + tile * size.forced + row
    return folded[pl.ds(start, count * size.each, stride=tiles * size.forced), :]


def start_points(point_refs, ints, floats, sems):
    copies = []
    for index, ref in enumerate(point_refs):
        target = (ints if index < 2 else floats).at[index % 2]
        copy = pltpu.make_async_copy(ref, target, sems.at[index])
        copy.start()
        copies.append(copy)
    return copies


def block_stencil(size, me, block, first_tile, ints, floats, right_hi, right_lo):
    center, diffuse = zone_factors(size.forced)
    window = 2 * LANES
    lanes = pl.ds(pl.multiple_of(first_tile * LANES, LANES), window)
    zone = ints.shape[1]
    lane = lax.broadcasted_iota(jnp.int32, (zone, window), 1)
    third = divided_by_3(first_tile * LANES + lane)
    first_col = first_columns(ints[0, :, lanes], third, me * size.par, size.total) - block * size.bw
    col_weights = lagrange_weights(floats[0, :, lanes])
    row_weights = lagrange_weights(floats[1, :, lanes])
    first_row = ints[1, :, lanes]

    def shifted(value, shift):
        if shift == 0:
            return value
        return pltpu.roll(value, (-shift) % window, 1)

    column = lax.broadcasted_iota(jnp.int32, (size.bw, LANES), 0)
    prow = lax.broadcasted_iota(jnp.int32, (8, LANES), 0)
    source = {}
    for shift in (-1, 0, 1):
        base = shifted(first_col, shift)
        if shift == -1:
            base = jnp.where(lane == 0, FAR, base)
        if shift == 1:
            base = jnp.where(lane == window - 1, FAR, base)
        source[shift] = (
            base,
            [shifted(w, shift) for w in col_weights],
            shifted(first_row, shift),
            [shifted(w, shift) for w in row_weights],
        )
    for half in range(2):
        part = slice(half * LANES, (half + 1) * LANES)
        tables = {}
        for row in range(size.forced):
            for zone_row, shift, _ in diffused_terms(row, size.forced, center, diffuse):
                if (zone_row, shift) in tables:
                    continue
                base, col_w, base_row, row_w = source[shift]
                one = slice(zone_row, zone_row + 1)
                tables[zone_row, shift] = (
                    tap_select(column - base[one, part], [w[one, part] for w in col_w]),
                    tap_select(prow - base_row[one, part], [w[one, part] for w in row_w]),
                )
        for row in range(size.forced):
            terms = [
                (tables[zone_row, shift][0], tables[zone_row, shift][1] * factor)
                for zone_row, shift, factor in diffused_terms(row, size.forced, center, diffuse)
            ]
            depth = slice(row * window + half * LANES, row * window + (half + 1) * LANES)
            for pair in range(PROWS // 2):
                pieces = []
                for p in (2 * pair, 2 * pair + 1):
                    products = [col_w * row_w[p : p + 1] for col_w, row_w in terms]
                    pieces.append(functools.reduce(jnp.add, products))
                high, low = split_bf16(jnp.concatenate(pieces, axis=0))
                rows = slice(2 * pair * size.bw, 2 * (pair + 1) * size.bw)
                right_hi[rows, depth] = high
                right_lo[rows, depth] = low


def spill_hits(size, entry, column, at_left, at_right):
    side = (entry // SPILL_ROWS) & 1
    inner = entry & (SPILL_ROWS - 1)
    target = (inner >> 2) * size.bw + (inner & 3)
    on_left = (side == 0) & at_left & (column == target)
    on_right = (side == 1) & at_right & (column == target + size.bw - SPILL)
    return jnp.where((inner < PROWS * SPILL) & (on_left | on_right), 1.0, 0.0).astype(jnp.bfloat16)


def block_of(size, owner_ref, dest):
    block = jnp.int32(0)
    for candidate in range(size.tiles):
        block = block + jnp.where(owner_ref[0, candidate] == dest, candidate, 0)
    return block


def pack_rest(size, rest, out_ref):
    rest = jnp.concatenate([rest, jnp.zeros((size.lead, LANES - size.rest), jnp.float32)], axis=1)
    for octet in range(size.rest_octets):
        packed = None
        for member in range(size.share):
            index = member * size.rest_octets + octet
            if index >= size.octets:
                continue
            piece = rest[8 * index : 8 * index + 8]
            if member:
                piece = pltpu.roll(piece, member * size.rest, 1)
            packed = piece if packed is None else packed + piece
        start = size.full * size.lead + 8 * octet
        out_ref[start : start + 8] = packed


def product(left, right_hi, right_lo):
    contract = (((1,), (1,)), ((), ()))
    count = left.shape[0] // 2
    both = lax.dot_general(left, right_hi, contract, preferred_element_type=jnp.float32)
    extra = lax.dot_general(left[:count], right_lo, contract, preferred_element_type=jnp.float32)
    return both[:count] + both[count:] + extra


def window_of(size, block):
    first = jnp.maximum(3 * size.bw * block - 10, 0) // LANES
    return jnp.minimum(first, size.point_tiles - 2)


def first_call(size, step, owner, cotangent, points):
    zone = points[0].shape[0]
    window = 2 * LANES
    depth = size.forced * window
    chunks = ((0, size.fields - 2), (size.fields - 2, size.fields))

    def kernel(owner_hbm, cot_ref, *refs):
        point_refs, out_ref, edge_refs, refs = refs[:4], refs[4], refs[5:7], refs[7:]
        owner_ref, owner_sem, buffer, folded, sems, ints, floats, point_sems, left, right_hi, right_lo = refs[:-3]
        edge_buffer, edge_folded, edge_sems = refs[-3:]
        owner_copy = pltpu.make_async_copy(owner_hbm, owner_ref, owner_sem)
        owner_copy.start()
        point_copies = start_points(point_refs, ints, floats, point_sems)
        edge_copies = []
        for end, tile in enumerate((0, size.point_tiles - 1)):
            copy = pltpu.make_async_copy(
                cot_ref.at[:, :, :, pl.ds(tile, 1)], edge_buffer.at[:, :, :, pl.ds(end, 1)], edge_sems.at[end]
            )
            copy.start()
            edge_copies.append(copy)
        me = lax.axis_index("tile")
        owner_copy.wait()
        block = block_of(size, owner_ref, me ^ step)
        first_tile = window_of(size, block)
        copies = []
        for field in range(size.fields):
            copy = pltpu.make_async_copy(
                cot_ref.at[:, field, :, pl.ds(first_tile, 2)], buffer.at[field], sems.at[field]
            )
            copy.start()
            copies.append(copy)
        for copy in point_copies:
            copy.wait()
        center, diffuse = zone_factors(size.forced)
        lane = lax.broadcasted_iota(jnp.int32, (zone, LANES), 1)
        entry = lax.broadcasted_iota(jnp.int32, (SPILL_ROWS, LANES), 0)
        entry_lane = lax.broadcasted_iota(jnp.int32, (SPILL_ROWS, LANES), 1)
        parent_row = entry >> 2
        stencils = []
        for tile, edge_lane, out_start in ((0, 0, -SPILL), (size.point_tiles - 1, LANES - 1, size.par)):
            part = slice(tile * LANES, (tile + 1) * LANES)
            third = divided_by_3(tile * LANES + lane)
            first_col = first_columns(ints[0, :, part], third, me * size.par, size.total)
            own = [first_col, ints[1, :, part]]
            own += lagrange_weights(floats[0, :, part]) + lagrange_weights(floats[1, :, part])
            source = {0: own}
            for shift in (-1, 1):
                moved = [pltpu.roll(value, (-shift) % LANES, 1) for value in own]
                moved[0] = jnp.where(lane == (0 if shift == -1 else LANES - 1), FAR, moved[0])
                source[shift] = moved

            def one(values, row):
                rows = [value[row : row + 1] for value in values]
                along = tap_select((entry & 3) + out_start - rows[0], rows[2:6])
                across = tap_select(parent_row - rows[1], rows[6:10])
                return along * across

            stencil = []
            for row in range(size.forced):
                terms = [
                    one(source[shift], zone_row) * factor
                    for zone_row, shift, factor in diffused_terms(row, size.forced, center, diffuse)
                ]
                picks = (entry == PROWS * SPILL + row - 1) & (entry_lane == edge_lane) & (row > 0)
                stencil.append(jnp.where(picks, 1.0, functools.reduce(jnp.add, terms)))
            stencils.append(jnp.concatenate(stencil, axis=1))

        for copy in edge_copies:
            copy.wait()
        for field in range(size.fields):
            fold_field(size, field, 2, edge_buffer, edge_folded, steps_first=True)
        contract = (((1,), (1,)), ((), ()))
        for end in range(2):
            parts = []
            for row in range(size.forced):
                values = folded_rows(size, edge_folded, 0, size.fields, 2, end, row)
                parts.append(jnp.concatenate(split_bf16(values), axis=0))
            right = jnp.concatenate(parts, axis=1)
            high, low = split_bf16(stencils[end])
            both = lax.dot_general(high, right, contract, preferred_element_type=jnp.float32)
            extra = lax.dot_general(low, right[: size.lead], contract, preferred_element_type=jnp.float32)
            edge_ref = edge_refs[end]
            edge_ref[...] = jnp.zeros((EDGE_ROWS, size.wide), jnp.float32)
            edge_ref[:SPILL_ROWS, : size.lead] = both[:, : size.lead] + both[:, size.lead :] + extra
            point = 0 if end == 0 else size.seg - 1
            start = PROWS * SPILL + size.forced - 1
            for kind in range(4):
                for row in range(1, size.forced):
                    value = (ints if kind < 2 else floats)[kind % 2, row : row + 1, point : point + 1]
                    edge_ref[start : start + 1] = jnp.broadcast_to(value.astype(jnp.float32), (1, size.wide))
                    start += 1
        block_stencil(size, me, block, first_tile, ints, floats, right_hi, right_lo)
        pieces = []
        for first, last in chunks:
            for field in range(first, last):
                copies[field].wait()
                fold_field(size, field, 2, buffer, folded)
            base, count = 2 * first * size.each, (last - first) * size.each
            for half in range(2):
                for row in range(size.forced):
                    high, low = split_bf16(folded_rows(size, folded, first, last - first, 2, half, row))
                    part = slice(row * window + half * LANES, row * window + (half + 1) * LANES)
                    left[base : base + count, part] = high
                    left[base + count : base + 2 * count, part] = low
            result = product(left[base : base + 2 * count], right_hi[...], right_lo[...])
            for tile in range(size.full):
                start = tile * size.lead + first * size.each
                out_ref[start : start + count] = result[:, tile * LANES : (tile + 1) * LANES]
            pieces.append(result[:, size.full * LANES :])
        pack_rest(size, jnp.concatenate(pieces, axis=0), out_ref)

    vmem = pl.BlockSpec(memory_space=pltpu.VMEM)
    hbm = pl.BlockSpec(memory_space=pltpu.HBM)
    return pl.pallas_call(
        kernel,
        out_shape=[pltpu.VMEM((size.packed, LANES), jnp.float32)]
        + [pltpu.VMEM((EDGE_ROWS, size.wide), jnp.float32)] * 2,
        in_specs=[hbm] * 6,
        out_specs=[vmem] * 3,
        scratch_shapes=[pltpu.SMEM((1, size.tiles), jnp.int32), pltpu.SemaphoreType.DMA]
        + size.fold_scratch(2)
        + size.point_scratch(zone)
        + [
            pltpu.VMEM((2 * size.lead, depth), jnp.bfloat16),
            pltpu.VMEM((size.cols, depth), jnp.bfloat16),
            pltpu.VMEM((size.cols, depth), jnp.bfloat16),
            pltpu.VMEM((size.steps, size.fields, size.levels, 2, size.forced, LANES), jnp.float32),
            pltpu.VMEM((size.lead * 2 * size.forced, LANES), jnp.float32),
            pltpu.SemaphoreType.DMA((2,)),
        ],
        compiler_params=pltpu.CompilerParams(vmem_limit_bytes=VMEM_BYTES),
        name=f"block_{step}",
    )(in_hbm(owner), in_hbm(cotangent), *map(in_hbm, points))


def write_blocks(size, steps, owner_ref, parts_ref, ints, floats, across_ref, out_refs, right_hi, right_lo):
    inner = size.forced * 2 * LANES
    me = lax.axis_index("tile")
    for step, out_ref in zip(steps, out_refs):
        block = block_of(size, owner_ref, me ^ step)
        first_tile = window_of(size, block)
        block_stencil(size, me, block, first_tile, ints, floats, right_hi, right_lo)
        left = [
            parts_ref[first_tile + half, row] for row in range(size.forced) for half in range(2)
        ]
        left.append(across_ref[...])
        column = lax.broadcasted_iota(jnp.int32, (size.cols, LANES), 0)
        entry = lax.broadcasted_iota(jnp.int32, (size.cols, LANES), 1)
        right_hi[:, inner:] = spill_hits(size, entry, column, block == 0, block == size.tiles - 1)
        right_lo[:, inner:] = jnp.zeros((size.cols, LANES), jnp.bfloat16)
        result = product(jnp.concatenate(left, axis=1), right_hi[...], right_lo[...])
        for tile in range(size.full):
            start = tile * size.lead
            out_ref[start : start + size.lead] = result[:, tile * LANES : (tile + 1) * LANES]
        pack_rest(size, result[:, size.full * LANES :], out_ref)


def block_call(size, steps, owner, parts, ints, floats, across, fix=None, after=(), unread=()):
    depth = size.forced * 2 * LANES + LANES

    def kernel(owner_ref, parts_ref, ints, floats, across_ref, *refs):
        if fix is not None:
            fix_ref, refs = refs[0], refs[1:]
        refs = refs[len(after) + len(unread) :]
        out_refs, refs = refs[: len(steps)], refs[len(steps) :]
        if fix is not None:
            refs[0][...] = fix_ref[...]
            refs = refs[1:]
        right_hi, right_lo = refs
        write_blocks(size, steps, owner_ref, parts_ref, ints, floats, across_ref, out_refs, right_hi, right_lo)

    vmem = pl.BlockSpec(memory_space=pltpu.VMEM)
    operands = [parts, ints, floats, across] + ([] if fix is None else [fix]) + list(after)
    outs = [pltpu.VMEM((size.packed, LANES), jnp.float32)] * len(steps)
    if fix is not None:
        outs.append(pltpu.VMEM((SPILL_ROWS, size.wide), jnp.float32))
    return pl.pallas_call(
        kernel,
        out_shape=outs,
        in_specs=[pl.BlockSpec(memory_space=pltpu.SMEM)]
        + [vmem] * len(operands)
        + [pl.BlockSpec(memory_space=pltpu.HBM)] * len(unread),
        out_specs=[vmem] * len(outs),
        scratch_shapes=[pltpu.VMEM((size.cols, depth), jnp.bfloat16)] * 2,
        compiler_params=pltpu.CompilerParams(vmem_limit_bytes=BLOCK_VMEM),
        name="block_" + "_".join(map(str, steps)),
    )(owner, *map(in_vmem, operands), *map(in_hbm, unread))


def in_vmem(array):
    return pltpu.with_memory_space_constraint(array, pltpu.VMEM)


def in_hbm(array):
    return pltpu.with_memory_space_constraint(array, pltpu.HBM)


def fold_call(size, cotangent, points, after):
    zone = points[0].shape[0]

    def kernel(cot_ref, *refs):
        point_refs, parts_ref, ints, floats, buffer, folded, sems, point_sems = refs[:4], *refs[4 + len(after) :]
        point_copies = start_points(point_refs, ints, floats, point_sems)
        copies = []
        for field in range(size.fields):
            copy = pltpu.make_async_copy(cot_ref.at[:, field], buffer.at[field], sems.at[field])
            copy.start()
            copies.append(copy)
        for copy in point_copies:
            copy.wait()
        for field in range(size.fields):
            copies[field].wait()
            fold_field(size, field, size.point_tiles, buffer, folded)
            rows = slice(field * size.each, (field + 1) * size.each)
            low_rows = slice(size.lead + field * size.each, size.lead + (field + 1) * size.each)
            for tile in range(size.point_tiles):
                for row in range(size.forced):
                    values = folded_rows(size, folded, field, 1, size.point_tiles, tile, row)
                    parts_ref[tile, row, rows], parts_ref[tile, row, low_rows] = split_bf16(values)

    vmem = pl.BlockSpec(memory_space=pltpu.VMEM)
    hbm = pl.BlockSpec(memory_space=pltpu.HBM)
    return pl.pallas_call(
        kernel,
        out_shape=[
            pltpu.VMEM((size.point_tiles, size.forced, 2 * size.lead, LANES), jnp.bfloat16),
            pltpu.VMEM((2, zone, size.seg), jnp.int32),
            pltpu.VMEM((2, zone, size.seg), jnp.float32),
        ],
        in_specs=[hbm] * 5 + [vmem] * len(after),
        out_specs=[vmem] * 3,
        scratch_shapes=size.fold_scratch(size.point_tiles) + size.point_scratch(zone)[2:],
        compiler_params=pltpu.CompilerParams(vmem_limit_bytes=VMEM_BYTES),
        name="fold",
    )(in_hbm(cotangent), *map(in_hbm, points), *map(in_vmem, after))


def join_call(size, early, step, owner, edges, from_left, from_right, parts, ints, floats):
    depth = size.forced * 2 * LANES + LANES

    def kernel(owner_ref, *refs):
        left_ref, right_ref, from_left_ref, from_right_ref, parts_ref, ints, floats = refs[:7]
        across_ref, fix_ref, out_ref, right_hi, right_lo = refs[7:]
        me = lax.axis_index("tile")
        _, diffuse = zone_factors(size.forced)
        entry = lax.broadcasted_iota(jnp.int32, (SPILL_ROWS, size.wide), 0)
        spills = []
        for own_ref, other_ref, own_point, other_third, first in (
            (left_ref, from_left_ref, 0, -1, 0),
            (right_ref, from_right_ref, size.seg - 1, size.par, size.par - SPILL),
        ):
            total = other_ref[:SPILL_ROWS]
            column = (entry & 3) + first
            for row in range(1, size.forced):
                start = PROWS * SPILL + size.forced - 1

                def stencil(ref, third):
                    kinds = [
                        ref[start + kind * (size.forced - 1) + row - 1 :][:1] for kind in range(4)
                    ]
                    cols = kinds[0].astype(jnp.int32)
                    base = first_columns(cols, jnp.full_like(cols, third), me * size.par, size.total)
                    along = tap_select(column - base, lagrange_weights(kinds[2]))
                    across = tap_select((entry >> 2) - kinds[1].astype(jnp.int32), lagrange_weights(kinds[3]))
                    return along * across

                folded_row = PROWS * SPILL + row - 1
                here = stencil(own_ref, own_point // 3) * other_ref[folded_row : folded_row + 1]
                there = stencil(other_ref, other_third) * own_ref[folded_row : folded_row + 1]
                total = total - diffuse[row] * (here + there)
            spills.append(jnp.where(entry < PROWS * SPILL, total, 0.0))
        blank = jnp.zeros((LANES - 2 * SPILL_ROWS, size.wide), jnp.float32)
        across = jnp.transpose(jnp.concatenate(spills + [blank], axis=0))[: size.lead]
        across_ref[: size.lead], across_ref[size.lead :] = split_bf16(across)
        fixed = block_of(size, owner_ref, me ^ early)
        fix = jnp.where(fixed == 0, spills[0], jnp.where(fixed == size.tiles - 1, spills[1], 0.0))
        flag = jnp.where(fixed == 0, 1.0, 0.0)
        fix_ref[...] = jnp.where(entry == SPILL_ROWS - 1, flag, fix)
        write_blocks(
            size, [step], owner_ref, parts_ref, ints, floats, across_ref, [out_ref], right_hi, right_lo
        )

    vmem = pl.BlockSpec(memory_space=pltpu.VMEM)
    return pl.pallas_call(
        kernel,
        out_shape=[
            pltpu.VMEM((2 * size.lead, LANES), jnp.bfloat16),
            pltpu.VMEM((SPILL_ROWS, size.wide), jnp.float32),
            pltpu.VMEM((size.packed, LANES), jnp.float32),
        ],
        in_specs=[pl.BlockSpec(memory_space=pltpu.SMEM)] + [vmem] * 7,
        out_specs=[vmem] * 3,
        scratch_shapes=[pltpu.VMEM((size.cols, depth), jnp.bfloat16)] * 2,
        compiler_params=pltpu.CompilerParams(vmem_limit_bytes=BLOCK_VMEM),
        name="join",
    )(owner, *map(in_vmem, [*edges, from_left, from_right, parts, ints, floats]))


def hand_on(value, after):
    def kernel(value_ref, *refs):
        refs[-1][...] = value_ref[...]

    vmem = pl.BlockSpec(memory_space=pltpu.VMEM)
    return pl.pallas_call(
        kernel,
        out_shape=pltpu.VMEM(value.shape, jnp.float32),
        in_specs=[vmem] * (1 + len(after)),
        out_specs=vmem,
        name="hand_on",
    )(in_vmem(value), *map(in_vmem, after))


def fix_call(size, block, fix, after):
    def kernel(block_ref, fix_ref, _, out_ref):
        values = fix_ref[...]
        values = jnp.concatenate(
            [values, jnp.zeros((LANES - SPILL_ROWS, size.wide), jnp.float32)], axis=0
        )
        across = jnp.transpose(values)[: size.lead]
        at_left = fix_ref[SPILL_ROWS - 1, 0] > 0.5
        column = lax.broadcasted_iota(jnp.int32, (size.cols, LANES), 0)
        entry = lax.broadcasted_iota(jnp.int32, (size.cols, LANES), 1)
        hits = [
            spill_hits(size, entry + SPILL_ROWS * side, column, side == 0, side == 1) for side in range(2)
        ]
        inside = entry < SPILL_ROWS
        right = jnp.where(at_left, hits[0].astype(jnp.float32), hits[1].astype(jnp.float32))
        right = jnp.where(inside, right, 0.0).astype(jnp.bfloat16)
        high, low = split_bf16(across)
        contract = (((1,), (1,)), ((), ()))
        both = lax.dot_general(
            jnp.concatenate([high, low], axis=0), right, contract, preferred_element_type=jnp.float32
        )
        result = both[: size.lead] + both[size.lead :]
        for tile in range(size.full):
            rows = slice(tile * size.lead, (tile + 1) * size.lead)
            out_ref[rows] = block_ref[rows] + result[:, tile * LANES : (tile + 1) * LANES]
        rows = slice(size.full * size.lead, size.packed)
        pack_rest(size, result[:, size.full * LANES :], out_ref)
        out_ref[rows] += block_ref[rows]

    vmem = pl.BlockSpec(memory_space=pltpu.VMEM)
    return pl.pallas_call(
        kernel,
        out_shape=pltpu.VMEM((size.packed, LANES), jnp.float32),
        in_specs=[vmem] * 3,
        out_specs=vmem,
        compiler_params=pltpu.CompilerParams(vmem_limit_bytes=VMEM_BYTES),
        name="fix",
    )(in_vmem(block), in_vmem(fix), in_vmem(after))


def pieces(size, source, member):
    for p in range(PROWS):
        done = 0
        while done < size.bw:
            from_lane = p * size.bw + done
            to_lane = source * size.bw + done
            count = min(size.bw - done, LANES - from_lane % LANES, LANES - to_lane % LANES)
            held = from_lane // LANES
            extra = member * size.rest if held == size.full else 0
            start = to_lane % LANES
            yield p, to_lane // LANES, start, start + count, held, (to_lane - from_lane - extra) % LANES
            done += count


def each_octet(size, one_octet):
    def body(i, carry):
        for member in range(size.share):
            octet = member * size.rest_octets + i
            if (member + 1) * size.rest_octets <= size.octets:
                one_octet(octet, member)
            else:
                pl.when(octet < size.octets)(functools.partial(one_octet, octet, member))
        return carry

    lax.fori_loop(0, size.rest_octets, body, 0)


def octet_rows(size, octet, member):
    rows = [pl.ds(pl.multiple_of(tile * size.lead + 8 * octet, 8), 8) for tile in range(size.full)]
    start = size.full * size.lead + 8 * (octet - member * size.rest_octets)
    return rows + [pl.ds(pl.multiple_of(start, 8), 8)]


def octet_pairs(size, octet):
    per_octet = 8 // size.levels
    field = octet // (NT // per_octet)
    time = per_octet * (octet - field * (NT // per_octet))
    return [(time + k) * size.fields + field for k in range(per_octet)]


def merge(size, refs, position, octet, member, merged):
    lane = lax.broadcasted_iota(jnp.int32, (8, LANES), 1)
    rows = octet_rows(size, octet, member)
    for source in range(size.tiles):
        if source ^ position not in refs:
            continue
        tiles = [refs[source ^ position][r] for r in rows]
        for p, tile, start, stop, held, shift in pieces(size, source, member):
            value = pltpu.roll(tiles[held], shift, 1) if shift else tiles[held]
            if (p, tile) in merged:
                value = jnp.where((lane >= start) & (lane < stop), value, merged[p, tile])
            merged[p, tile] = value


def at_position(size, one_octet):
    me = lax.axis_index("tile")
    for position in range(size.tiles):
        pl.when(me == position)(functools.partial(each_octet, size, functools.partial(one_octet, position)))


def place_call(size, arrived, unread):
    shape = (size.octets, PROWS, size.par // LANES, 8, LANES)

    def kernel(*refs):
        blocks, staged = dict(zip(arrived, refs)), refs[-1]

        def one_octet(position, octet, member):
            merged = {}
            merge(size, blocks, position, octet, member, merged)
            for (p, tile), value in merged.items():
                staged[octet, p, tile] = value

        at_position(size, one_octet)

    vmem = pl.BlockSpec(memory_space=pltpu.VMEM)
    return pl.pallas_call(
        kernel,
        out_shape=pltpu.VMEM(shape, jnp.float32),
        in_specs=[vmem] * len(arrived) + [pl.BlockSpec(memory_space=pltpu.HBM)],
        out_specs=vmem,
        compiler_params=pltpu.CompilerParams(vmem_limit_bytes=BLOCK_VMEM),
        name="place",
    )(*map(in_vmem, arrived.values()), in_hbm(unread))


def finish_call(size, staged, arrived):
    shape = (NT * size.fields, PROWS, size.levels, size.par)

    def kernel(staged_ref, *refs):
        blocks, (out_ref, final, sem) = dict(zip(arrived, refs)), refs[len(arrived) :]

        def one_octet(position, octet, member):
            merged = {
                (p, tile): staged_ref[octet, p, tile]
                for p in range(PROWS)
                for tile in range(size.par // LANES)
            }
            merge(size, blocks, position, octet, member, merged)
            for k, pair in enumerate(octet_pairs(size, octet)):
                for (p, tile), value in merged.items():
                    part = slice(tile * LANES, (tile + 1) * LANES)
                    final[pair, p, :, part] = value[k * size.levels : (k + 1) * size.levels]
                pltpu.make_async_copy(final.at[pair], out_ref.at[pair], sem).start()

        at_position(size, one_octet)
        pltpu.make_async_copy(final, out_ref, sem).wait()

    vmem = pl.BlockSpec(memory_space=pltpu.VMEM)
    return pl.pallas_call(
        kernel,
        out_shape=jax.ShapeDtypeStruct(shape, jnp.float32),
        in_specs=[vmem] * (1 + len(arrived)),
        out_specs=pl.BlockSpec(memory_space=pltpu.HBM),
        scratch_shapes=[pltpu.VMEM(shape, jnp.float32), pltpu.SemaphoreType.DMA],
        compiler_params=pltpu.CompilerParams(vmem_limit_bytes=BLOCK_VMEM),
        name="finish",
    )(in_vmem(staged), *map(in_vmem, arrived.values()))


def more_call(size, staged, arrived, unread):
    shape = staged.shape

    def kernel(*refs):
        blocks, staged_ref = dict(zip(arrived, refs[1:])), refs[-1]

        def one_octet(position, octet, member):
            touched = {
                source ^ position: [
                    (p, tile) for p, tile, *_ in pieces(size, source, member)
                ]
                for source in range(size.tiles)
                if source ^ position in blocks
            }
            merged = {
                (p, tile): staged_ref[octet, p, tile] for keys in touched.values() for p, tile in keys
            }
            merge(size, blocks, position, octet, member, merged)
            for (p, tile), value in merged.items():
                staged_ref[octet, p, tile] = value

        at_position(size, one_octet)

    vmem = pl.BlockSpec(memory_space=pltpu.VMEM)
    return pl.pallas_call(
        kernel,
        out_shape=pltpu.VMEM(shape, jnp.float32),
        in_specs=[vmem] * (1 + len(arrived)) + [pl.BlockSpec(memory_space=pltpu.HBM)],
        out_specs=vmem,
        input_output_aliases={0: 0},
        compiler_params=pltpu.CompilerParams(vmem_limit_bytes=BLOCK_VMEM),
        name="more",
    )(in_vmem(staged), *map(in_vmem, arrived.values()), in_hbm(unread))


def shards(cotangent, stencil_col, stencil_row, frac_along, frac_across, owner_map):
    tiles = lax.axis_size("tile")
    size = Sizes(cotangent.shape, tiles)
    points = (stencil_col, stencil_row, frac_along, frac_across)
    up = [(i, (i + 1) % tiles) for i in range(tiles)]
    down = [(j, i) for i, j in up]
    tiled = cotangent.reshape(cotangent.shape[:-1] + (size.point_tiles, LANES))
    tiled = jnp.transpose(tiled, (0, 1, 2, 4, 3, 5))
    half = tiles // 2
    far, near = list(range(half, tiles)), list(range(half - 1, 0, -1))
    arrived = [None] * tiles

    def send(step, value):
        return lax.ppermute(value, "tile", [(i, i ^ step) for i in range(tiles)])

    early = far[0]
    first, *edges = first_call(size, early, owner_map, tiled, points)
    arrived[early] = send(early, first)
    from_right = lax.ppermute(edges[0], "tile", down)
    from_left = lax.ppermute(edges[1], "tile", up)
    parts, ints, floats = fold_call(size, tiled, points, edges)
    across, fix, block = join_call(
        size, early, far[1], owner_map, edges, from_left, from_right, parts, ints, floats
    )
    arrived[far[1]] = send(far[1], block)
    turns = [kind[i : i + 2] for kind in (far[2:], near) for i in range(0, len(kind), 2)]
    made = block_call(size, far[2:] + near, owner_map, parts, ints, floats, across, None, [block])
    for step, block in zip(far[2:] + near, made):
        arrived[step] = send(step, block)
    arrived[0] = block_call(
        size, [0], owner_map, parts, ints, floats, across, None, [made[0], arrived[early]]
    )[0]
    fix = send(early, hand_on(fix, [arrived[0]]))
    staged = place_call(size, {step: arrived[step] for step in (far[1], 0)}, tiled)
    for turn in turns[:-1]:
        staged = more_call(size, staged, {step: arrived[step] for step in turn}, tiled)
    arrived[early] = fix_call(size, arrived[early], fix, staged)
    placed = finish_call(size, staged, {step: arrived[step] for step in turns[-1] + [early]})
    placed = placed.reshape(NT, size.fields, PROWS, size.levels, size.par)
    return jnp.transpose(placed, (0, 1, 3, 2, 4))


def solution(mesh):
    in_specs = (
        P(None, None, "lev", None, ("ens", "tile")),
        P(None, ("ens", "tile")),
        P(None, ("ens", "tile")),
        P(None, ("ens", "tile")),
        P(None, ("ens", "tile")),
        P(("ens", "tile"), None),
    )
    out_specs = P(None, None, "lev", None, ("ens", "tile"))
    return jax.shard_map(shards, mesh=mesh, in_specs=in_specs, out_specs=out_specs, check_vma=False)
```

```python
import functools

import jax
import jax.numpy as jnp
from jax import lax
from jax.experimental import pallas as pl
from jax.experimental.pallas import tpu as pltpu
from jax.sharding import PartitionSpec as P

PROWS = 6
NT = 12
STEPS_PER = 3
LANES = 128
TAPS = 4
SPILL = 4
SPILL_ROWS = 32
EDGE_ROWS = 40
FAR = -(1 << 20)
VMEM_BYTES = 28 << 20
BLOCK_VMEM = 16 << 20


def zone_factors(forced):
    relax = [0.0] + [(forced - r) / (forced - 1.0) for r in range(1, forced)]
    diffuse = [0.2 * value for value in relax]
    center = [1.0] + [relax[r] + 4.0 * diffuse[r] for r in range(1, forced)]
    return center, diffuse


def lagrange_weights(fraction):
    shifted = fraction + 1.0
    return [
        -fraction * (fraction - 1.0) * (fraction - 2.0) / 6.0,
        shifted * (fraction - 1.0) * (fraction - 2.0) / 2.0,
        -shifted * fraction * (fraction - 2.0) / 2.0,
        shifted * fraction * (fraction - 1.0) / 6.0,
    ]


def split_bf16(value):
    high = value.astype(jnp.bfloat16)
    low = (value - high.astype(jnp.float32)).astype(jnp.bfloat16)
    return high, low


def tap_select(distance, weights):
    picked = jnp.where(distance == TAPS - 1, weights[TAPS - 1], 0.0)
    for tap in range(TAPS - 2, -1, -1):
        picked = jnp.where(distance == tap, weights[tap], picked)
    return picked


def first_columns(cols, third, tile_start, total):
    offset = cols - (tile_start + third)
    offset = jnp.where(offset < -2, offset + total, offset)
    offset = jnp.where(offset > 0, offset - total, offset)
    return third + offset


def divided_by_3(value):
    return (value * 21846) >> 16


def diffused_terms(row, forced, center, diffuse):
    terms = [(row, 0, center[row])]
    if diffuse[row] != 0.0:
        terms += [(row, -1, -diffuse[row]), (row, 1, -diffuse[row])]
        terms += [(row + 1, 0, -diffuse[row]), (row - 1, 0, -diffuse[row])]
    return terms


def fold_times(read, write, steps):
    values = {}

    def value(t):
        if t not in values:
            values[t] = read(t)
        return values[t]

    for k in range(NT):
        total = value(STEPS_PER * k)
        for gap in range(1, STEPS_PER):
            near = [value(t) for t in (STEPS_PER * k - gap, STEPS_PER * k + gap) if 0 <= t < steps]
            total = total + (1.0 - gap / STEPS_PER) * functools.reduce(jnp.add, near)
        write(k, total)


class Sizes:
    def __init__(self, cotangent_shape, tile_count):
        self.steps, self.fields, self.levels, self.forced, self.seg = cotangent_shape
        self.tiles = tile_count
        self.par = self.seg // 3
        self.total = self.par * tile_count
        self.bw = self.par // tile_count
        self.each = NT * self.levels
        self.lead = self.fields * self.each
        self.cols = PROWS * self.bw
        self.full = self.cols // LANES
        self.rest = self.cols % LANES
        self.share = LANES // self.rest
        self.octets = self.lead // 8
        self.rest_octets = -(-self.octets // self.share)
        self.packed = self.full * self.lead + 8 * self.rest_octets
        self.point_tiles = self.seg // LANES
        self.wide = -(-self.lead // LANES) * LANES

    def fold_scratch(self, tiles):
        rows = self.levels * tiles * self.forced
        return [
            pltpu.VMEM((self.fields, self.steps, self.levels, tiles, self.forced, LANES), jnp.float32),
            pltpu.VMEM((self.fields * NT * rows, LANES), jnp.float32),
            pltpu.SemaphoreType.DMA((self.fields,)),
        ]

    def point_scratch(self, zone):
        return [
            pltpu.VMEM((2, zone, self.seg), jnp.int32),
            pltpu.VMEM((2, zone, self.seg), jnp.float32),
            pltpu.SemaphoreType.DMA((4,)),
        ]


def fold_field(size, field, tiles, buffer, folded, steps_first=False):
    rows = size.levels * tiles * size.forced
    flat = buffer.reshape(*buffer.shape[:2], rows, LANES)

    def one_part(index, carry):
        part = pl.multiple_of(16 * index, 16)

        def write(k, value):
            start = (field * NT + k) * rows
            folded[pl.ds(start + part, 16), :] = value

        fold_times(
            lambda t: flat[t, field, pl.ds(part, 16)] if steps_first else flat[field, t, pl.ds(part, 16)],
            write,
            size.steps,
        )
        return carry

    lax.fori_loop(0, rows // 16, one_part, 0)


def folded_rows(size, folded, first_field, count, tiles, tile, row):
    rows = size.levels * tiles * size.forced
    start = first_field * NT * rows + tile * size.forced + row
    return folded[pl.ds(start, count * size.each, stride=tiles * size.forced), :]


def start_points(point_refs, ints, floats, sems):
    copies = []
    for index, ref in enumerate(point_refs):
        target = (ints if index < 2 else floats).at[index % 2]
        copy = pltpu.make_async_copy(ref, target, sems.at[index])
        copy.start()
        copies.append(copy)
    return copies


def block_stencil(size, me, block, first_tile, ints, floats, right_hi, right_lo):
    center, diffuse = zone_factors(size.forced)
    window = 2 * LANES
    lanes = pl.ds(pl.multiple_of(first_tile * LANES, LANES), window)
    zone = ints.shape[1]
    lane = lax.broadcasted_iota(jnp.int32, (zone, window), 1)
    third = divided_by_3(first_tile * LANES + lane)
    first_col = first_columns(ints[0, :, lanes], third, me * size.par, size.total) - block * size.bw
    col_weights = lagrange_weights(floats[0, :, lanes])
    row_weights = lagrange_weights(floats[1, :, lanes])
    first_row = ints[1, :, lanes]

    def shifted(value, shift):
        if shift == 0:
            return value
        return pltpu.roll(value, (-shift) % window, 1)

    column = lax.broadcasted_iota(jnp.int32, (size.bw, LANES), 0)
    prow = lax.broadcasted_iota(jnp.int32, (8, LANES), 0)
    source = {}
    for shift in (-1, 0, 1):
        base = shifted(first_col, shift)
        if shift == -1:
            base = jnp.where(lane == 0, FAR, base)
        if shift == 1:
            base = jnp.where(lane == window - 1, FAR, base)
        source[shift] = (
            base,
            [shifted(w, shift) for w in col_weights],
            shifted(first_row, shift),
            [shifted(w, shift) for w in row_weights],
        )
    for half in range(2):
        part = slice(half * LANES, (half + 1) * LANES)
        tables = {}
        for row in range(size.forced):
            for zone_row, shift, _ in diffused_terms(row, size.forced, center, diffuse):
                if (zone_row, shift) in tables:
                    continue
                base, col_w, base_row, row_w = source[shift]
                one = slice(zone_row, zone_row + 1)
                tables[zone_row, shift] = (
                    tap_select(column - base[one, part], [w[one, part] for w in col_w]),
                    tap_select(prow - base_row[one, part], [w[one, part] for w in row_w]),
                )
        for row in range(size.forced):
            terms = [
                (tables[zone_row, shift][0], tables[zone_row, shift][1] * factor)
                for zone_row, shift, factor in diffused_terms(row, size.forced, center, diffuse)
            ]
            depth = slice(row * window + half * LANES, row * window + (half + 1) * LANES)
            for pair in range(PROWS // 2):
                pieces = []
                for p in (2 * pair, 2 * pair + 1):
                    products = [col_w * row_w[p : p + 1] for col_w, row_w in terms]
                    pieces.append(functools.reduce(jnp.add, products))
                high, low = split_bf16(jnp.concatenate(pieces, axis=0))
                rows = slice(2 * pair * size.bw, 2 * (pair + 1) * size.bw)
                right_hi[rows, depth] = high
                right_lo[rows, depth] = low


def spill_hits(size, entry, column, at_left, at_right):
    side = (entry // SPILL_ROWS) & 1
    inner = entry & (SPILL_ROWS - 1)
    target = (inner >> 2) * size.bw + (inner & 3)
    on_left = (side == 0) & at_left & (column == target)
    on_right = (side == 1) & at_right & (column == target + size.bw - SPILL)
    return jnp.where((inner < PROWS * SPILL) & (on_left | on_right), 1.0, 0.0).astype(jnp.bfloat16)


def block_of(size, owner_ref, dest):
    block = jnp.int32(0)
    for candidate in range(size.tiles):
        block = block + jnp.where(owner_ref[0, candidate] == dest, candidate, 0)
    return block


def pack_rest(size, rest, out_ref):
    rest = jnp.concatenate([rest, jnp.zeros((size.lead, LANES - size.rest), jnp.float32)], axis=1)
    for octet in range(size.rest_octets):
        packed = None
        for member in range(size.share):
            index = member * size.rest_octets + octet
            if index >= size.octets:
                continue
            piece = rest[8 * index : 8 * index + 8]
            if member:
                piece = pltpu.roll(piece, member * size.rest, 1)
            packed = piece if packed is None else packed + piece
        start = size.full * size.lead + 8 * octet
        out_ref[start : start + 8] = packed


def product(left, right_hi, right_lo):
    contract = (((1,), (1,)), ((), ()))
    count = left.shape[0] // 2
    both = lax.dot_general(left, right_hi, contract, preferred_element_type=jnp.float32)
    extra = lax.dot_general(left[:count], right_lo, contract, preferred_element_type=jnp.float32)
    return both[:count] + both[count:] + extra


def window_of(size, block):
    first = jnp.maximum(3 * size.bw * block - 10, 0) // LANES
    return jnp.minimum(first, size.point_tiles - 2)


def first_call(size, step, owner, cotangent, points):
    zone = points[0].shape[0]
    window = 2 * LANES
    depth = size.forced * window
    chunks = ((0, size.fields - 2), (size.fields - 2, size.fields))

    def kernel(owner_hbm, cot_ref, *refs):
        point_refs, out_ref, edge_refs, refs = refs[:4], refs[4], refs[5:7], refs[7:]
        owner_ref, owner_sem, buffer, folded, sems, ints, floats, point_sems, left, right_hi, right_lo = refs[:-3]
        edge_buffer, edge_folded, edge_sems = refs[-3:]
        owner_copy = pltpu.make_async_copy(owner_hbm, owner_ref, owner_sem)
        owner_copy.start()
        point_copies = start_points(point_refs, ints, floats, point_sems)
        edge_copies = []
        for end, tile in enumerate((0, size.point_tiles - 1)):
            copy = pltpu.make_async_copy(
                cot_ref.at[:, :, :, pl.ds(tile, 1)], edge_buffer.at[:, :, :, pl.ds(end, 1)], edge_sems.at[end]
            )
            copy.start()
            edge_copies.append(copy)
        me = lax.axis_index("tile")
        owner_copy.wait()
        block = block_of(size, owner_ref, me ^ step)
        first_tile = window_of(size, block)
        copies = []
        for field in range(size.fields):
            copy = pltpu.make_async_copy(
                cot_ref.at[:, field, :, pl.ds(first_tile, 2)], buffer.at[field], sems.at[field]
            )
            copy.start()
            copies.append(copy)
        for copy in point_copies:
            copy.wait()
        block_stencil(size, me, block, first_tile, ints, floats, right_hi, right_lo)
        center, diffuse = zone_factors(size.forced)
        lane = lax.broadcasted_iota(jnp.int32, (zone, LANES), 1)
        entry = lax.broadcasted_iota(jnp.int32, (SPILL_ROWS, LANES), 0)
        entry_lane = lax.broadcasted_iota(jnp.int32, (SPILL_ROWS, LANES), 1)
        parent_row = entry >> 2
        stencils = []
        for tile, edge_lane, out_start in ((0, 0, -SPILL), (size.point_tiles - 1, LANES - 1, size.par)):
            part = slice(tile * LANES, (tile + 1) * LANES)
            third = divided_by_3(tile * LANES + lane)
            first_col = first_columns(ints[0, :, part], third, me * size.par, size.total)
            own = [first_col, ints[1, :, part]]
            own += lagrange_weights(floats[0, :, part]) + lagrange_weights(floats[1, :, part])
            source = {0: own}
            for shift in (-1, 1):
                moved = [pltpu.roll(value, (-shift) % LANES, 1) for value in own]
                moved[0] = jnp.where(lane == (0 if shift == -1 else LANES - 1), FAR, moved[0])
                source[shift] = moved

            def one(values, row):
                rows = [value[row : row + 1] for value in values]
                along = tap_select((entry & 3) + out_start - rows[0], rows[2:6])
                across = tap_select(parent_row - rows[1], rows[6:10])
                return along * across

            stencil = []
            for row in range(size.forced):
                terms = [
                    one(source[shift], zone_row) * factor
                    for zone_row, shift, factor in diffused_terms(row, size.forced, center, diffuse)
                ]
                picks = (entry == PROWS * SPILL + row - 1) & (entry_lane == edge_lane) & (row > 0)
                stencil.append(jnp.where(picks, 1.0, functools.reduce(jnp.add, terms)))
            stencils.append(jnp.concatenate(stencil, axis=1))

        for copy in edge_copies:
            copy.wait()
        for field in range(size.fields):
            fold_field(size, field, 2, edge_buffer, edge_folded, steps_first=True)
        contract = (((1,), (1,)), ((), ()))
        for end in range(2):
            parts = []
            for row in range(size.forced):
                values = folded_rows(size, edge_folded, 0, size.fields, 2, end, row)
                parts.append(jnp.concatenate(split_bf16(values), axis=0))
            right = jnp.concatenate(parts, axis=1)
            high, low = split_bf16(stencils[end])
            both = lax.dot_general(high, right, contract, preferred_element_type=jnp.float32)
            extra = lax.dot_general(low, right[: size.lead], contract, preferred_element_type=jnp.float32)
            edge_ref = edge_refs[end]
            edge_ref[...] = jnp.zeros((EDGE_ROWS, size.wide), jnp.float32)
            edge_ref[:SPILL_ROWS, : size.lead] = both[:, : size.lead] + both[:, size.lead :] + extra
            point = 0 if end == 0 else size.seg - 1
            start = PROWS * SPILL + size.forced - 1
            for kind in range(4):
                for row in range(1, size.forced):
                    value = (ints if kind < 2 else floats)[kind % 2, row : row + 1, point : point + 1]
                    edge_ref[start : start + 1] = jnp.broadcast_to(value.astype(jnp.float32), (1, size.wide))
                    start += 1
        pieces = []
        for first, last in chunks:
            for field in range(first, last):
                copies[field].wait()
                fold_field(size, field, 2, buffer, folded)
            base, count = 2 * first * size.each, (last - first) * size.each
            for half in range(2):
                for row in range(size.forced):
                    high, low = split_bf16(folded_rows(size, folded, first, last - first, 2, half, row))
                    part = slice(row * window + half * LANES, row * window + (half + 1) * LANES)
                    left[base : base + count, part] = high
                    left[base + count : base + 2 * count, part] = low
            result = product(left[base : base + 2 * count], right_hi[...], right_lo[...])
            for tile in range(size.full):
                start = tile * size.lead + first * size.each
                out_ref[start : start + count] = result[:, tile * LANES : (tile + 1) * LANES]
            pieces.append(result[:, size.full * LANES :])
        pack_rest(size, jnp.concatenate(pieces, axis=0), out_ref)

    vmem = pl.BlockSpec(memory_space=pltpu.VMEM)
    hbm = pl.BlockSpec(memory_space=pltpu.HBM)
    return pl.pallas_call(
        kernel,
        out_shape=[pltpu.VMEM((size.packed, LANES), jnp.float32)]
        + [pltpu.VMEM((EDGE_ROWS, size.wide), jnp.float32)] * 2,
        in_specs=[hbm] * 6,
        out_specs=[vmem] * 3,
        scratch_shapes=[pltpu.SMEM((1, size.tiles), jnp.int32), pltpu.SemaphoreType.DMA]
        + size.fold_scratch(2)
        + size.point_scratch(zone)
        + [
            pltpu.VMEM((2 * size.lead, depth), jnp.bfloat16),
            pltpu.VMEM((size.cols, depth), jnp.bfloat16),
            pltpu.VMEM((size.cols, depth), jnp.bfloat16),
            pltpu.VMEM((size.steps, size.fields, size.levels, 2, size.forced, LANES), jnp.float32),
            pltpu.VMEM((size.lead * 2 * size.forced, LANES), jnp.float32),
            pltpu.SemaphoreType.DMA((2,)),
        ],
        compiler_params=pltpu.CompilerParams(vmem_limit_bytes=VMEM_BYTES),
        name=f"block_{step}",
    )(in_hbm(owner), in_hbm(cotangent), *map(in_hbm, points))


def write_blocks(size, steps, owner_ref, parts_ref, ints, floats, across_ref, out_refs, right_hi, right_lo):
    inner = size.forced * 2 * LANES
    me = lax.axis_index("tile")
    for step, out_ref in zip(steps, out_refs):
        block = block_of(size, owner_ref, me ^ step)
        first_tile = window_of(size, block)
        block_stencil(size, me, block, first_tile, ints, floats, right_hi, right_lo)
        left = [
            parts_ref[first_tile + half, row] for row in range(size.forced) for half in range(2)
        ]
        left.append(across_ref[...])
        column = lax.broadcasted_iota(jnp.int32, (size.cols, LANES), 0)
        entry = lax.broadcasted_iota(jnp.int32, (size.cols, LANES), 1)
        right_hi[:, inner:] = spill_hits(size, entry, column, block == 0, block == size.tiles - 1)
        right_lo[:, inner:] = jnp.zeros((size.cols, LANES), jnp.bfloat16)
        result = product(jnp.concatenate(left, axis=1), right_hi[...], right_lo[...])
        for tile in range(size.full):
            start = tile * size.lead
            out_ref[start : start + size.lead] = result[:, tile * LANES : (tile + 1) * LANES]
        pack_rest(size, result[:, size.full * LANES :], out_ref)


def block_call(size, steps, owner, parts, ints, floats, across, fix=None, after=(), unread=()):
    depth = size.forced * 2 * LANES + LANES

    def kernel(owner_ref, parts_ref, ints, floats, across_ref, *refs):
        if fix is not None:
            fix_ref, refs = refs[0], refs[1:]
        refs = refs[len(after) + len(unread) :]
        out_refs, refs = refs[: len(steps)], refs[len(steps) :]
        if fix is not None:
            refs[0][...] = fix_ref[...]
            refs = refs[1:]
        right_hi, right_lo = refs
        write_blocks(size, steps, owner_ref, parts_ref, ints, floats, across_ref, out_refs, right_hi, right_lo)

    vmem = pl.BlockSpec(memory_space=pltpu.VMEM)
    operands = [parts, ints, floats, across] + ([] if fix is None else [fix]) + list(after)
    outs = [pltpu.VMEM((size.packed, LANES), jnp.float32)] * len(steps)
    if fix is not None:
        outs.append(pltpu.VMEM((SPILL_ROWS, size.wide), jnp.float32))
    return pl.pallas_call(
        kernel,
        out_shape=outs,
        in_specs=[pl.BlockSpec(memory_space=pltpu.SMEM)]
        + [vmem] * len(operands)
        + [pl.BlockSpec(memory_space=pltpu.HBM)] * len(unread),
        out_specs=[vmem] * len(outs),
        scratch_shapes=[pltpu.VMEM((size.cols, depth), jnp.bfloat16)] * 2,
        compiler_params=pltpu.CompilerParams(vmem_limit_bytes=BLOCK_VMEM),
        name="block_" + "_".join(map(str, steps)),
    )(owner, *map(in_vmem, operands), *map(in_hbm, unread))


def in_vmem(array):
    return pltpu.with_memory_space_constraint(array, pltpu.VMEM)


def in_hbm(array):
    return pltpu.with_memory_space_constraint(array, pltpu.HBM)


def fold_call(size, cotangent, points, after):
    zone = points[0].shape[0]

    def kernel(cot_ref, *refs):
        point_refs, parts_ref, ints, floats, buffer, folded, sems, point_sems = refs[:4], *refs[4 + len(after) :]
        point_copies = start_points(point_refs, ints, floats, point_sems)
        copies = []
        for field in range(size.fields):
            copy = pltpu.make_async_copy(cot_ref.at[:, field], buffer.at[field], sems.at[field])
            copy.start()
            copies.append(copy)
        for copy in point_copies:
            copy.wait()
        for field in range(size.fields):
            copies[field].wait()
            fold_field(size, field, size.point_tiles, buffer, folded)
            rows = slice(field * size.each, (field + 1) * size.each)
            low_rows = slice(size.lead + field * size.each, size.lead + (field + 1) * size.each)
            for tile in range(size.point_tiles):
                for row in range(size.forced):
                    values = folded_rows(size, folded, field, 1, size.point_tiles, tile, row)
                    parts_ref[tile, row, rows], parts_ref[tile, row, low_rows] = split_bf16(values)

    vmem = pl.BlockSpec(memory_space=pltpu.VMEM)
    hbm = pl.BlockSpec(memory_space=pltpu.HBM)
    return pl.pallas_call(
        kernel,
        out_shape=[
            pltpu.VMEM((size.point_tiles, size.forced, 2 * size.lead, LANES), jnp.bfloat16),
            pltpu.VMEM((2, zone, size.seg), jnp.int32),
            pltpu.VMEM((2, zone, size.seg), jnp.float32),
        ],
        in_specs=[hbm] * 5 + [vmem] * len(after),
        out_specs=[vmem] * 3,
        scratch_shapes=size.fold_scratch(size.point_tiles) + size.point_scratch(zone)[2:],
        compiler_params=pltpu.CompilerParams(vmem_limit_bytes=VMEM_BYTES),
        name="fold",
    )(in_hbm(cotangent), *map(in_hbm, points), *map(in_vmem, after))


def join_call(size, early, step, owner, edges, from_left, from_right, parts, ints, floats):
    depth = size.forced * 2 * LANES + LANES

    def kernel(owner_ref, *refs):
        left_ref, right_ref, from_left_ref, from_right_ref, parts_ref, ints, floats = refs[:7]
        across_ref, fix_ref, out_ref, right_hi, right_lo = refs[7:]
        me = lax.axis_index("tile")
        _, diffuse = zone_factors(size.forced)
        entry = lax.broadcasted_iota(jnp.int32, (SPILL_ROWS, size.wide), 0)
        spills = []
        for own_ref, other_ref, own_point, other_third, first in (
            (left_ref, from_left_ref, 0, -1, 0),
            (right_ref, from_right_ref, size.seg - 1, size.par, size.par - SPILL),
        ):
            total = other_ref[:SPILL_ROWS]
            column = (entry & 3) + first
            for row in range(1, size.forced):
                start = PROWS * SPILL + size.forced - 1

                def stencil(ref, third):
                    kinds = [
                        ref[start + kind * (size.forced - 1) + row - 1 :][:1] for kind in range(4)
                    ]
                    cols = kinds[0].astype(jnp.int32)
                    base = first_columns(cols, jnp.full_like(cols, third), me * size.par, size.total)
                    along = tap_select(column - base, lagrange_weights(kinds[2]))
                    across = tap_select((entry >> 2) - kinds[1].astype(jnp.int32), lagrange_weights(kinds[3]))
                    return along * across

                folded_row = PROWS * SPILL + row - 1
                here = stencil(own_ref, own_point // 3) * other_ref[folded_row : folded_row + 1]
                there = stencil(other_ref, other_third) * own_ref[folded_row : folded_row + 1]
                total = total - diffuse[row] * (here + there)
            spills.append(jnp.where(entry < PROWS * SPILL, total, 0.0))
        blank = jnp.zeros((LANES - 2 * SPILL_ROWS, size.wide), jnp.float32)
        across = jnp.transpose(jnp.concatenate(spills + [blank], axis=0))[: size.lead]
        across_ref[: size.lead], across_ref[size.lead :] = split_bf16(across)
        fixed = block_of(size, owner_ref, me ^ early)
        fix = jnp.where(fixed == 0, spills[0], jnp.where(fixed == size.tiles - 1, spills[1], 0.0))
        flag = jnp.where(fixed == 0, 1.0, 0.0)
        lane = lax.broadcasted_iota(jnp.int32, fix.shape, 1)
        fix_ref[...] = jnp.where(lane == size.wide - 1, flag, fix)[: PROWS * SPILL]
        write_blocks(
            size, [step], owner_ref, parts_ref, ints, floats, across_ref, [out_ref], right_hi, right_lo
        )

    vmem = pl.BlockSpec(memory_space=pltpu.VMEM)
    return pl.pallas_call(
        kernel,
        out_shape=[
            pltpu.VMEM((2 * size.lead, LANES), jnp.bfloat16),
            pltpu.VMEM((PROWS * SPILL, size.wide), jnp.float32),
            pltpu.VMEM((size.packed, LANES), jnp.float32),
        ],
        in_specs=[pl.BlockSpec(memory_space=pltpu.SMEM)] + [vmem] * 7,
        out_specs=[vmem] * 3,
        scratch_shapes=[pltpu.VMEM((size.cols, depth), jnp.bfloat16)] * 2,
        compiler_params=pltpu.CompilerParams(vmem_limit_bytes=BLOCK_VMEM),
        name="join",
    )(owner, *map(in_vmem, [*edges, from_left, from_right, parts, ints, floats]))


def hand_on(value, after):
    def kernel(value_ref, *refs):
        refs[-1][...] = value_ref[...]

    vmem = pl.BlockSpec(memory_space=pltpu.VMEM)
    return pl.pallas_call(
        kernel,
        out_shape=pltpu.VMEM(value.shape, jnp.float32),
        in_specs=[vmem] * (1 + len(after)),
        out_specs=vmem,
        name="hand_on",
    )(in_vmem(value), *map(in_vmem, after))


def fix_call(size, block, fix, after):
    def kernel(block_ref, fix_ref, _, out_ref):
        values = fix_ref[...]
        values = jnp.concatenate(
            [values, jnp.zeros((LANES - PROWS * SPILL, size.wide), jnp.float32)], axis=0
        )
        across = jnp.transpose(values)[: size.lead]
        at_left = fix_ref[0, size.wide - 1] > 0.5
        column = lax.broadcasted_iota(jnp.int32, (size.cols, LANES), 0)
        entry = lax.broadcasted_iota(jnp.int32, (size.cols, LANES), 1)
        hits = [
            spill_hits(size, entry + SPILL_ROWS * side, column, side == 0, side == 1) for side in range(2)
        ]
        inside = entry < SPILL_ROWS
        right = jnp.where(at_left, hits[0].astype(jnp.float32), hits[1].astype(jnp.float32))
        right = jnp.where(inside, right, 0.0).astype(jnp.bfloat16)
        high, low = split_bf16(across)
        contract = (((1,), (1,)), ((), ()))
        both = lax.dot_general(
            jnp.concatenate([high, low], axis=0), right, contract, preferred_element_type=jnp.float32
        )
        result = both[: size.lead] + both[size.lead :]
        for tile in range(size.full):
            rows = slice(tile * size.lead, (tile + 1) * size.lead)
            out_ref[rows] = block_ref[rows] + result[:, tile * LANES : (tile + 1) * LANES]
        rows = slice(size.full * size.lead, size.packed)
        pack_rest(size, result[:, size.full * LANES :], out_ref)
        out_ref[rows] += block_ref[rows]

    vmem = pl.BlockSpec(memory_space=pltpu.VMEM)
    return pl.pallas_call(
        kernel,
        out_shape=pltpu.VMEM((size.packed, LANES), jnp.float32),
        in_specs=[vmem] * 3,
        out_specs=vmem,
        compiler_params=pltpu.CompilerParams(vmem_limit_bytes=VMEM_BYTES),
        name="fix",
    )(in_vmem(block), in_vmem(fix), in_vmem(after))


def pieces(size, source, member):
    for p in range(PROWS):
        done = 0
        while done < size.bw:
            from_lane = p * size.bw + done
            to_lane = source * size.bw + done
            count = min(size.bw - done, LANES - from_lane % LANES, LANES - to_lane % LANES)
            held = from_lane // LANES
            extra = member * size.rest if held == size.full else 0
            start = to_lane % LANES
            yield p, to_lane // LANES, start, start + count, held, (to_lane - from_lane - extra) % LANES
            done += count


def each_octet(size, one_octet):
    def body(i, carry):
        for member in range(size.share):
            octet = member * size.rest_octets + i
            if (member + 1) * size.rest_octets <= size.octets:
                one_octet(octet, member)
            else:
                pl.when(octet < size.octets)(functools.partial(one_octet, octet, member))
        return carry

    lax.fori_loop(0, size.rest_octets, body, 0)


def octet_rows(size, octet, member):
    rows = [pl.ds(pl.multiple_of(tile * size.lead + 8 * octet, 8), 8) for tile in range(size.full)]
    start = size.full * size.lead + 8 * (octet - member * size.rest_octets)
    return rows + [pl.ds(pl.multiple_of(start, 8), 8)]


def octet_pairs(size, octet):
    per_octet = 8 // size.levels
    field = octet // (NT // per_octet)
    time = per_octet * (octet - field * (NT // per_octet))
    return [(time + k) * size.fields + field for k in range(per_octet)]


def merge(size, refs, position, octet, member, merged):
    lane = lax.broadcasted_iota(jnp.int32, (8, LANES), 1)
    rows = octet_rows(size, octet, member)
    for source in range(size.tiles):
        if source ^ position not in refs:
            continue
        tiles = [refs[source ^ position][r] for r in rows]
        for p, tile, start, stop, held, shift in pieces(size, source, member):
            value = pltpu.roll(tiles[held], shift, 1) if shift else tiles[held]
            if (p, tile) in merged:
                value = jnp.where((lane >= start) & (lane < stop), value, merged[p, tile])
            merged[p, tile] = value


def at_position(size, one_octet):
    me = lax.axis_index("tile")
    for position in range(size.tiles):
        pl.when(me == position)(functools.partial(each_octet, size, functools.partial(one_octet, position)))


def place_call(size, arrived, unread):
    shape = (size.octets, PROWS, size.par // LANES, 8, LANES)

    def kernel(*refs):
        blocks, staged = dict(zip(arrived, refs)), refs[-1]

        def one_octet(position, octet, member):
            merged = {}
            merge(size, blocks, position, octet, member, merged)
            for (p, tile), value in merged.items():
                staged[octet, p, tile] = value

        at_position(size, one_octet)

    vmem = pl.BlockSpec(memory_space=pltpu.VMEM)
    return pl.pallas_call(
        kernel,
        out_shape=pltpu.VMEM(shape, jnp.float32),
        in_specs=[vmem] * len(arrived) + [pl.BlockSpec(memory_space=pltpu.HBM)],
        out_specs=vmem,
        compiler_params=pltpu.CompilerParams(vmem_limit_bytes=BLOCK_VMEM),
        name="place",
    )(*map(in_vmem, arrived.values()), in_hbm(unread))


def finish_call(size, staged, arrived):
    shape = (NT * size.fields, PROWS, size.levels, size.par)

    def kernel(staged_ref, *refs):
        blocks, (out_ref, final, sem) = dict(zip(arrived, refs)), refs[len(arrived) :]

        def one_octet(position, octet, member):
            merged = {
                (p, tile): staged_ref[octet, p, tile]
                for p in range(PROWS)
                for tile in range(size.par // LANES)
            }
            merge(size, blocks, position, octet, member, merged)
            for k, pair in enumerate(octet_pairs(size, octet)):
                for (p, tile), value in merged.items():
                    part = slice(tile * LANES, (tile + 1) * LANES)
                    final[pair, p, :, part] = value[k * size.levels : (k + 1) * size.levels]
                pltpu.make_async_copy(final.at[pair], out_ref.at[pair], sem).start()

        at_position(size, one_octet)
        pltpu.make_async_copy(final, out_ref, sem).wait()

    vmem = pl.BlockSpec(memory_space=pltpu.VMEM)
    return pl.pallas_call(
        kernel,
        out_shape=jax.ShapeDtypeStruct(shape, jnp.float32),
        in_specs=[vmem] * (1 + len(arrived)),
        out_specs=pl.BlockSpec(memory_space=pltpu.HBM),
        scratch_shapes=[pltpu.VMEM(shape, jnp.float32), pltpu.SemaphoreType.DMA],
        compiler_params=pltpu.CompilerParams(vmem_limit_bytes=BLOCK_VMEM),
        name="finish",
    )(in_vmem(staged), *map(in_vmem, arrived.values()))


def more_call(size, staged, arrived, unread):
    shape = staged.shape

    def kernel(*refs):
        blocks, staged_ref = dict(zip(arrived, refs[1:])), refs[-1]

        def one_octet(position, octet, member):
            touched = {
                source ^ position: [
                    (p, tile) for p, tile, *_ in pieces(size, source, member)
                ]
                for source in range(size.tiles)
                if source ^ position in blocks
            }
            merged = {
                (p, tile): staged_ref[octet, p, tile] for keys in touched.values() for p, tile in keys
            }
            merge(size, blocks, position, octet, member, merged)
            for (p, tile), value in merged.items():
                staged_ref[octet, p, tile] = value

        at_position(size, one_octet)

    vmem = pl.BlockSpec(memory_space=pltpu.VMEM)
    return pl.pallas_call(
        kernel,
        out_shape=pltpu.VMEM(shape, jnp.float32),
        in_specs=[vmem] * (1 + len(arrived)) + [pl.BlockSpec(memory_space=pltpu.HBM)],
        out_specs=vmem,
        input_output_aliases={0: 0},
        compiler_params=pltpu.CompilerParams(vmem_limit_bytes=BLOCK_VMEM),
        name="more",
    )(in_vmem(staged), *map(in_vmem, arrived.values()), in_hbm(unread))


def shards(cotangent, stencil_col, stencil_row, frac_along, frac_across, owner_map):
    tiles = lax.axis_size("tile")
    size = Sizes(cotangent.shape, tiles)
    points = (stencil_col, stencil_row, frac_along, frac_across)
    up = [(i, (i + 1) % tiles) for i in range(tiles)]
    down = [(j, i) for i, j in up]
    tiled = cotangent.reshape(cotangent.shape[:-1] + (size.point_tiles, LANES))
    tiled = jnp.transpose(tiled, (0, 1, 2, 4, 3, 5))
    half = tiles // 2
    far, near = list(range(half, tiles)), list(range(half - 1, 0, -1))
    arrived = [None] * tiles

    def send(step, value):
        return lax.ppermute(value, "tile", [(i, i ^ step) for i in range(tiles)])

    early = far[0]
    first, *edges = first_call(size, early, owner_map, tiled, points)
    arrived[early] = send(early, first)
    from_right = lax.ppermute(edges[0], "tile", down)
    from_left = lax.ppermute(edges[1], "tile", up)
    parts, ints, floats = fold_call(size, tiled, points, edges)
    across, fix, block = join_call(
        size, early, far[1], owner_map, edges, from_left, from_right, parts, ints, floats
    )
    arrived[far[1]] = send(far[1], block)
    turns = [kind[i : i + 2] for kind in (far[2:], near) for i in range(0, len(kind), 2)]
    made = block_call(size, far[2:] + near, owner_map, parts, ints, floats, across, None, [block])
    for step, block in zip(far[2:] + near, made):
        arrived[step] = send(step, block)
    arrived[0] = block_call(
        size, [0], owner_map, parts, ints, floats, across, None, [made[0], arrived[early]]
    )[0]
    fix = send(early, hand_on(fix, [arrived[0]]))
    staged = place_call(size, {step: arrived[step] for step in (far[1], 0)}, tiled)
    for turn in turns[:-1]:
        staged = more_call(size, staged, {step: arrived[step] for step in turn}, tiled)
    arrived[early] = fix_call(size, arrived[early], fix, staged)
    placed = finish_call(size, staged, {step: arrived[step] for step in turns[-1] + [early]})
    placed = placed.reshape(NT, size.fields, PROWS, size.levels, size.par)
    return jnp.transpose(placed, (0, 1, 3, 2, 4))


def solution(mesh):
    in_specs = (
        P(None, None, "lev", None, ("ens", "tile")),
        P(None, ("ens", "tile")),
        P(None, ("ens", "tile")),
        P(None, ("ens", "tile")),
        P(None, ("ens", "tile")),
        P(("ens", "tile"), None),
    )
    out_specs = P(None, None, "lev", None, ("ens", "tile"))
    return jax.shard_map(shards, mesh=mesh, in_specs=in_specs, out_specs=out_specs, check_vma=False)
```
